32 devices in a mesh: edge: 8 (over z, y), node: 4 (over x, core).
Axes of the slice: x: 2, y: 2, z: 4, core: 2. Of those that a mesh axis runs over, the one named last changes fastest.
Arguments:
- residual: float32 [64, 32768], P(None, ('edge', 'node')), may hold values from -6 to 6
- tangent: float32 [3, 64, 32768], P(None, None, ('edge', 'node')), may hold values from -4 to 4
- jacobi: float32 [64, 32768], P(None, ('edge', 'node')), may hold values from 0.2 to 1
- ends: int32 [2, 64, 32768], P(None, None, ('edge', 'node')), may hold values from 0 to 31, as said below
- target: int32 [32768, 1], P(('edge', 'node')), may hold values from 0 to 31; in each aligned block of 1024 rows (0 to 1023, 1024 to 2047, ...) at most 64 rows name the same one
- node_block: int32 [32768], P(('edge', 'node')), may hold values from 0 to 1023
- sigma: float32 [128, 32, 256], P(('edge', 'node')), may hold values from 0.25 to 8
Outputs:
- correction: float32 [64, 32768], P(None, ('edge', 'node'))
The draws below stay inside these ranges and needn't reach their ends.
Inputs may be any that keep to these rules, and one draw needn't show every extreme that they name: `ends`: the head and tail of an edge differ. `target`: among the 1024 rows of one device no device is named more than 64 times, and one is named exactly 64 times.
All inputs are finite; a program needn't handle non-finite values.
Results may differ from the reference program's by a relative error of at most 0.000086.
Values sent between devices are 32-bit elements; how exact they have to be, the bound alone decides.
A program may use at most 64 MiB of HBM per device.

```python
import math
import jax
import jax.numpy as jnp
import numpy as np

BLOCK_EDGES = 64
NODE_BLOCK = 32
R = 32
Z = 256
NBD = 1024
EBD = 1024
CAP = 64
EBLOCKS = 32768
NA = 128
N_EDGE = 8
N_NODE = 4


def draw_ends(key, part):
    key = jax.random.fold_in(key, 11)
    first_key, second_key = jax.random.split(key)
    tail_end = jax.random.randint(first_key, (BLOCK_EDGES, EBLOCKS), 0, NODE_BLOCK)
    offset = jax.random.randint(second_key, (BLOCK_EDGES, EBLOCKS), 1, NODE_BLOCK)
    head_end = (tail_end + offset) % NODE_BLOCK
    return jnp.stack([tail_end, head_end], axis=0).astype(jnp.int32)


def touch_ends(entries, rng, least, top_value):
    spot = [jax.random.randint(jax.random.fold_in(rng, axis), (), 0, length) for axis, length in enumerate(entries.shape)]
    main_axis = entries.shape.index(max(entries.shape))
    beside = spot[:main_axis] + [(spot[main_axis] + 1) % entries.shape[main_axis]] + spot[main_axis + 1:]
    return entries.at[tuple(spot)].set(least).at[tuple(beside)].set(top_value)


def block_scale(own_key, shape, shards, least, largest):
    gain = 1.0
    for position, blocks in shards:
        draws = jax.random.uniform(jax.random.fold_in(jax.random.fold_in(own_key, 6), position), (blocks,), jnp.float32, least / len(shards), largest / len(shards))
        gain = gain * jnp.repeat(jnp.exp(draws), shape[position] // blocks).reshape((-1,) + (1,) * (len(shape) - 1 - position))
    return gain


def assign_block(key, own, number, rows, amount, top, bound, skew):
    sequence = jax.random.permutation(key, amount)
    heavy_load, common = portions_of(amount, rows * top, bound, skew, True), portions_of(amount, rows * top, bound, skew, False)
    places = jnp.arange(amount)

    def named(lengths, rotation):
        used = int((lengths > 0).sum())
        fixed = max(1, used // 4)
        moved = fixed + (places - fixed + rotation * (used - fixed)) % max(1, amount - fixed)
        return jnp.zeros((amount,), jnp.int32).at[sequence[jnp.where(places < fixed, places, moved)]].set(jnp.asarray(lengths, jnp.int32))

    lengths = jnp.where(number % 4 == 0, named(heavy_load, number // 4), named(common, number - number // 4 - 1))
    mixed = jax.random.permutation(jax.random.fold_in(own, 3), amount)
    source_of, receiver = mixed[0:amount // 2 * 2:2], mixed[1:amount // 2 * 2:2]
    room = jnp.minimum(lengths[source_of] - 1, bound - lengths[receiver]) // 2
    room = jnp.where((source_of == sequence[0]) | (receiver == sequence[0]) | (lengths[receiver] == 0), 0, jnp.maximum(room, 0))
    moved = jax.random.randint(jax.random.fold_in(own, 4), (amount // 2,), 0, 1 << 20) % (room + 1)
    lengths = lengths.at[source_of].add(-moved).at[receiver].add(moved)
    members = jnp.searchsorted(jnp.cumsum(lengths), jnp.arange(rows * top), side="right").astype(jnp.int32)
    listing = members.reshape(top, rows).T
    listing = listing[jax.random.permutation(jax.random.fold_in(own, 1), rows)]
    rotation = jax.random.randint(jax.random.fold_in(own, 2), (rows, 1), 0, top)
    return jnp.take_along_axis(listing, (jnp.arange(top)[None, :] + rotation) % top, axis=1)


def portions_of(number_of, total, limit, skew, full):
    loads = [(1 << 20) // math.isqrt(standing ** skew) + 1 for standing in range(1, number_of + 1)]
    largest = limit if full else min(limit, max(-(-total // number_of), total * loads[0] // sum(loads)))
    least = 1 if total - largest >= number_of - 1 else 0
    given, spare = [largest] + [least] * (number_of - 1), total - largest - least * (number_of - 1)
    while spare > 0:
        free = [i for i in range(1, number_of) if given[i] < largest] or [i for i in range(1, number_of) if given[i] < limit]
        mass, budget = sum([loads[i] for i in free]), spare
        for i in free:
            addition = min(limit - given[i], max(1, budget * loads[i] // mass), spare)
            given[i] = given[i] + addition
            spare = spare - addition
    return np.array(given)


def scatter_about(own_key, dims, deviation, bound, cuts=(), kind=jnp.bfloat16):
    drawn = jax.random.normal(own_key, dims, jnp.float32) * deviation
    if len(cuts) > 0:
        drawn = block_scale(own_key, dims, cuts, -0.22, 0.18) * drawn
    return jnp.clip(drawn, min=-bound, max=bound).astype(kind)


def setup_inputs(seed: int = 0) -> dict:
    arg_keys = jax.random.split(jax.random.key(seed), 8)
    residual = scatter_about(arg_keys[0], (BLOCK_EDGES, EBLOCKS), 1.0, 6.0, ((1, 32),), jnp.float32)
    tangent = scatter_about(arg_keys[1], (3, BLOCK_EDGES, EBLOCKS), 0.6, 4.0, ((2, 32),), jnp.float32)
    jacobi = jnp.clip(jnp.exp(math.log(1.0) - 1.609438 * jax.random.uniform(arg_keys[2], (BLOCK_EDGES, EBLOCKS), jnp.float32) ** block_scale(arg_keys[2], (BLOCK_EDGES, EBLOCKS), ((1, 32),), -0.2, 0.2)), 0.2, 1.0)
    ends = draw_ends(jax.random.fold_in(arg_keys[7], 71), 0)
    target_keys = jax.random.split(jax.random.fold_in(arg_keys[4], 1), EBLOCKS // EBD)
    target_turns = jax.random.permutation(jax.random.fold_in(arg_keys[4], 3), EBLOCKS // EBD)
    target = jax.vmap(lambda own, number: assign_block(jax.random.fold_in(arg_keys[4], 2), own, number, EBD, N_EDGE * N_NODE, 1, CAP, 2))(target_keys, target_turns).reshape((EBLOCKS, 1))
    node_block = touch_ends(jax.random.randint(arg_keys[5], (EBLOCKS,), 0, NBD), jax.random.fold_in(arg_keys[5], 1), 0, NBD - 1).astype(jnp.int32)
    sigma = jnp.clip(jnp.exp(math.log(8.0) - 3.465736 * jax.random.uniform(arg_keys[6], (NA, R, Z), jnp.float32) ** block_scale(arg_keys[6], (NA, R, Z), ((0, 32),), -0.2, 0.2)), 0.25, 8.0)
    return dict(residual=residual, tangent=tangent, jacobi=jacobi, ends=ends, target=target, node_block=node_block, sigma=sigma)


mass_scale = (1.0, 1.0, 1.0, 0.5)


def chebyshev_terms():
    scale = jnp.array(mass_scale, jnp.float32).reshape(4, 1, 1, 1)
    upper = 12.0 + 8.0 * scale
    lower = upper / 8.0
    centre = (upper + lower) / 2.0
    radius = (upper - lower) / 2.0
    ratio = centre / radius
    first = 1.0 / ratio
    second = 1.0 / (2.0 * ratio - first)
    return scale, centre, second * first, 2.0 * second / radius


def stiffness(padded, diag):
    centre = padded[:, 1:-1]
    beside_all = padded[:, :-2] + padded[:, 2:]
    inner = jnp.pad(centre, ((0, 0), (0, 0), (1, 1), (1, 1)))
    beside_all = beside_all + inner[:, :, :-2, 1:-1] + inner[:, :, 2:, 1:-1]
    beside_all = beside_all + inner[:, :, 1:-1, :-2] + inner[:, :, 1:-1, 2:]
    return diag * centre - beside_all


def wrapped(field):
    return jnp.concatenate([field[:, -1:], field, field[:, :1]], axis=1)


def reference(residual, tangent, jacobi, ends, target, node_block, sigma):
    scale, centre, coef_one, coef_two = chebyshev_terms()
    global_block = target[:, 0] * NBD + node_block
    base = global_block * NODE_BLOCK
    tail_node = (base[None, :] + ends[0]).reshape(-1)
    head_node = (base[None, :] + ends[1]).reshape(-1)
    node_count = NA * R * Z
    vector_terms = (0.5 * tangent * residual[None]).reshape(3, -1)
    flat_res = residual.reshape(-1)
    nodal_rhs = jnp.zeros((4, node_count), jnp.float32)
    nodal_rhs = nodal_rhs.at[:3, head_node].add(vector_terms)
    nodal_rhs = nodal_rhs.at[:3, tail_node].add(vector_terms)
    nodal_rhs = nodal_rhs.at[3, head_node].add(flat_res)
    nodal_rhs = nodal_rhs.at[3, tail_node].add(-flat_res)
    source = nodal_rhs.reshape(4, NA, R, Z)
    diag = 6.0 + scale * sigma[None]

    def apply(field):
        return stiffness(wrapped(field), diag)

    step_one = source / centre
    rest = source - apply(step_one)
    step_two = coef_one * step_one + coef_two * rest
    solution = step_one + step_two
    rest = source - apply(solution)
    step_one = rest / centre
    rest = rest - apply(step_one)
    step_two = coef_one * step_one + coef_two * rest
    solution = (solution + step_one) + step_two
    flat_sol = solution.reshape(4, -1)
    at_head = flat_sol[:, head_node].reshape(4, BLOCK_EDGES, -1)
    at_tail = flat_sol[:, tail_node].reshape(4, BLOCK_EDGES, -1)
    lifted = 0.5 * jnp.sum(tangent * (at_head[:3] + at_tail[:3]), axis=0)
    return jacobi * residual + lifted + (at_head[3] - at_tail[3])
```

```python
import functools

import jax
import jax.numpy as jnp
from jax import lax
from jax.experimental import pallas as pl
from jax.experimental.pallas import tpu as pltpu
from jax.sharding import PartitionSpec as P

BLOCK_EDGES = 64
NODE_BLOCK = 32
LANES = 128
GROUP = 256

F32 = jnp.float32
BF16 = jnp.bfloat16
MESH = pl.DeviceIdType.MESH


def halves(values):
    high = values.astype(BF16)
    low = (values - high.astype(F32)).astype(BF16)
    return high, low


def hot(mask):
    return jnp.where(mask, 1.0, 0.0).astype(BF16)


def dot(a, b):
    return jnp.dot(a, b, preferred_element_type=F32)


def folded(product):
    return product[:, :LANES] + product[:, LANES:]


def order_of(groups):
    return [(groups // 2 + 3 * k) % groups for k in range(groups)]


def kernel(
    n,
    n_node,
    slices,
    rows_radial,
    resid_ref,
    tangent_ref,
    jacobi_ref,
    ends_ref,
    target_ref,
    label_ref,
    diag_ref,
    out_ref,
    pos_ref,
    posb_ref,
    lab_out,
    lab_in,
    labb_ref,
    rows_ref,
    send_ref,
    got_ref,
    acc_ref,
    rest_ref,
    field_ref,
    sol_ref,
    back_ref,
    ret_ref,
    lab_send,
    lab_recv,
    go_send,
    go_recv,
    back_send,
    back_recv,
    halo_send,
    halo_recv,
):
    me = lax.axis_index("edge") * n_node + lax.axis_index("node")
    blocks = resid_ref.shape[1]
    lane_groups = blocks // LANES
    cap = 2 * blocks // n
    peers = GROUP // cap
    per_row = LANES // cap
    groups = n // peers
    my_group = me // peers
    my_place = lax.rem(me, peers)
    slab = rows_radial * 8
    nodal = slices * slab
    order = order_of(groups)

    def device(t):
        return (t // n_node, lax.rem(t, n_node))

    def to_group(step):
        return lax.rem(my_group + step, groups)

    def from_group(step):
        return lax.rem(my_group + groups - step, groups)

    def partner(group, turn):
        return group * peers + lax.rem(my_place + turn, peers)

    barrier = pltpu.get_barrier_semaphore()
    for step in range(1, n):
        pl.semaphore_signal(
            barrier, inc=1, device_id=device(lax.rem(me + step, n)), device_id_type=MESH
        )

    upper = hot(
        lax.broadcasted_iota(jnp.int32, (LANES, LANES), 0)
        <= lax.broadcasted_iota(jnp.int32, (LANES, LANES), 1)
    )
    device_ids = lax.broadcasted_iota(jnp.int32, (n, LANES), 0)
    slot_ids = lax.broadcasted_iota(jnp.int32, (LANES, LANES), 0)
    carry = jnp.zeros((n, 1), F32)
    label_sum = jnp.zeros((2 * n, LANES), F32)
    offset = lax.rem(me, per_row) * cap
    for g in range(lane_groups):
        cols = slice(g * LANES, (g + 1) * LANES)
        named = target_ref[:, cols]
        match = jnp.where(device_ids == named, 1.0, 0.0)
        local = dot(match.astype(BF16), upper)
        rank = jnp.sum(match * (local + carry), axis=0, keepdims=True) - 1.0
        carry = carry + local[:, LANES - 1 :]
        place = named * cap + rank.astype(jnp.int32)
        pos_ref[:, cols] = place
        posb_ref[cols, :] = jnp.broadcast_to(place.astype(F32), (LANES, LANES)).T
        mark = label_ref[:, cols] + 1
        high = match * (mark >> 5).astype(F32)
        low = match * (mark & 31).astype(F32)
        slots = hot(slot_ids == rank.astype(jnp.int32) + offset)
        label_sum = label_sum + lax.dot_general(
            jnp.concatenate([high, low], axis=0).astype(BF16),
            slots,
            (((1,), (1,)), ((), ())),
            preferred_element_type=F32,
        )
    labels = 32.0 * label_sum[:n] + label_sum[n:]
    for t in range(n):
        lab_out[t] = labels[t : t + 1]

    pl.semaphore_wait(barrier, n - 1)

    lab_in[me] = lab_out[me]
    for step in range(1, n):
        t = lax.rem(me + step, n)
        pltpu.make_async_remote_copy(
            src_ref=lab_out.at[t],
            dst_ref=lab_in.at[me],
            send_sem=lab_send,
            recv_sem=lab_recv,
            device_id=device(t),
            device_id_type=MESH,
        ).start()

    node_ids = lax.broadcasted_iota(jnp.int32, (NODE_BLOCK, LANES), 0)

    def terms_of(g, _):
        cols = pl.ds(pl.multiple_of(g * LANES, LANES), LANES)

        def chunk(k, sums):
            rows = pl.ds(pl.multiple_of(k * 8, 8), 8)
            residual = resid_ref[rows, cols]
            halved = 0.5 * residual
            vectors = [tangent_ref[c, rows, cols] * halved for c in range(3)]
            tails = ends_ref[0, rows, cols]
            heads = ends_ref[1, rows, cols]
            sums = list(sums)
            for e in range(8):
                at_tail = node_ids == tails[e : e + 1]
                at_head = node_ids == heads[e : e + 1]
                either = at_tail | at_head
                for c in range(3):
                    sums[c] = sums[c] + jnp.where(either, vectors[c][e : e + 1], 0.0)
                value = residual[e : e + 1]
                sums[3] = sums[3] + jnp.where(at_head, value, jnp.where(at_tail, -value, 0.0))
            return tuple(sums)

        zero = jnp.zeros((NODE_BLOCK, LANES), F32)
        sums = lax.fori_loop(0, BLOCK_EDGES // 8, chunk, (zero,) * 4)
        high, low = halves(jnp.concatenate(sums, axis=0).T)
        rows_ref[cols, :LANES] = high
        rows_ref[cols, LANES:] = low
        return 0

    lax.fori_loop(0, lane_groups, terms_of, 0)

    def rows_copy(src, dst, sends, recvs, step, turn):
        t = partner(to_group(step), turn)
        return pltpu.make_async_remote_copy(
            src_ref=src.at[pl.ds(pl.multiple_of(t * cap, cap), cap)],
            dst_ref=dst.at[pl.ds(pl.multiple_of(me * cap, cap), cap)],
            send_sem=sends.at[step],
            recv_sem=recvs.at[step],
            device_id=device(t),
            device_id_type=MESH,
        )

    def group_copy(src, dst, sends, recvs, step):
        size = GROUP if step else GROUP - cap
        return pltpu.make_async_remote_copy(
            src_ref=src.at[pl.ds(0, size)],
            dst_ref=dst.at[pl.ds(0, size)],
            send_sem=sends.at[step],
            recv_sem=recvs.at[step],
            device_id=device(me),
            device_id_type=MESH,
        )

    def send_group(src, dst, sends, recvs, step):
        for turn in range(peers):
            if step == 0 and turn == 0:
                mine = pl.ds(pl.multiple_of(me * cap, cap), cap)
                dst[mine, :] = src[mine, :]
            else:
                rows_copy(src, dst, sends, recvs, step, turn).start()

    for step in order:
        base = pl.multiple_of(to_group(step) * GROUP, GROUP)
        ids = lax.broadcasted_iota(jnp.int32, (GROUP, blocks), 0) + base
        send_ref[pl.ds(base, GROUP), :] = folded(dot(hot(pos_ref[...] == ids), rows_ref[...]))
        send_group(send_ref, got_ref, go_send, go_recv, step)

    pltpu.make_async_remote_copy(
        src_ref=lab_out.at[pl.ds(0, n - 1)],
        dst_ref=lab_in.at[pl.ds(0, n - 1)],
        send_sem=lab_send,
        recv_sem=lab_recv,
        device_id=device(me),
        device_id_type=MESH,
    ).wait()

    def label_row(first):
        total = lab_in[first]
        for k in range(1, per_row):
            total = total + lab_in[first + k]
        return total

    for k in range(2 * groups):
        row = label_row(k * per_row)
        labb_ref[k * LANES : (k + 1) * LANES, :] = jnp.broadcast_to(row, (LANES, LANES)).T

    block_ids = (lax.broadcasted_iota(jnp.int32, (nodal, LANES), 0) + 1).astype(F32)
    for k, step in enumerate(order):
        group_copy(send_ref, got_ref, go_send, go_recv, step).wait_recv()
        source = from_group(step)
        chosen = jnp.concatenate(
            [
                hot(block_ids == label_row(source * peers)),
                hot(block_ids == label_row(source * peers + per_row)),
            ],
            axis=1,
        )
        base = pl.multiple_of(source * GROUP, GROUP)
        high, low = halves(got_ref[pl.ds(base, GROUP), :])
        part = folded(dot(chosen, jnp.concatenate([high, low], axis=1)))
        acc_ref[...] = part if k == 0 else acc_ref[...] + part

    lane = lax.broadcasted_iota(jnp.int32, (1, LANES), 1)
    scale = jnp.where(lane < 3 * NODE_BLOCK, 1.0, 0.5).astype(F32)
    top = 12.0 + 8.0 * scale
    bottom = top / 8.0
    centre = (top + bottom) / 2.0
    radius = (top - bottom) / 2.0
    ratio = centre / radius
    first = 1.0 / ratio
    second = 1.0 / (2.0 * ratio - first)
    coef_one = second * first
    coef_two = 2.0 * second / radius
    inverse = 1.0 / centre

    inner = lax.broadcasted_iota(jnp.int32, (slab, LANES), 0) & 7
    node = lax.broadcasted_iota(jnp.int32, (slab, LANES), 1) & (NODE_BLOCK - 1)
    last_node = node == NODE_BLOCK - 1
    first_node = node == 0
    last_inner = inner == 7
    first_inner = inner == 0
    edge_zero = jnp.zeros((8, LANES), F32)
    left = lax.rem(me + n - 1, n)
    right = lax.rem(me + 1, n)

    def own(s):
        return slice(s * slab, (s + 1) * slab)

    def stored(s):
        return slice((s + 1) * slab, (s + 2) * slab)

    def halo(level, side):
        at = stored(0) if side == 0 else stored(slices - 1)
        to = stored(slices) if side == 0 else own(0)
        return pltpu.make_async_remote_copy(
            src_ref=field_ref.at[level, at],
            dst_ref=field_ref.at[level, to],
            send_sem=halo_send.at[level, side],
            recv_sem=halo_recv.at[level, side],
            device_id=device(left if side == 0 else right),
            device_id_type=MESH,
        )

    def applied(level, s):
        field = field_ref.at[level]
        here = field[stored(s)]
        beside = field[own(s)] + field[stored(s + 1)]
        beside = beside + jnp.concatenate([edge_zero, here[:-8]], axis=0)
        beside = beside + jnp.concatenate([here[8:], edge_zero], axis=0)
        after = pltpu.roll(pltpu.roll(here, slab - 1, 0), NODE_BLOCK - 1, 1)
        after = jnp.where(last_inner, 0.0, after)
        before = pltpu.roll(pltpu.roll(here, 1, 0), LANES - NODE_BLOCK + 1, 1)
        before = jnp.where(first_inner, 0.0, before)
        beside = beside + jnp.where(last_node, after, pltpu.roll(here, LANES - 1, 1))
        beside = beside + jnp.where(first_node, before, pltpu.roll(here, 1, 1))
        return diag_ref[own(s)] * here - beside

    outer = [0, slices - 1]
    middle = list(range(1, slices - 1))

    def stage(level, body):
        if level:
            for side in range(2):
                halo(level - 1, side).wait_recv()
        for s in outer:
            body(s)
        if level < 3:
            for side in range(2):
                halo(level, side).start()
        for s in middle:
            body(s)

    def begin(s):
        field_ref[0, stored(s)] = acc_ref[own(s)] * inverse

    def sweep(s):
        rest = acc_ref[own(s)] - applied(0, s)
        step = field_ref[0, stored(s)]
        field_ref[1, stored(s)] = step + (coef_one * step + coef_two * rest)

    def residue(s):
        rest = acc_ref[own(s)] - applied(1, s)
        rest_ref[own(s)] = rest
        field_ref[2, stored(s)] = rest * inverse

    def finish(s):
        step = field_ref[2, stored(s)]
        rest = rest_ref[own(s)] - applied(2, s)
        total = (field_ref[1, stored(s)] + step) + (coef_one * step + coef_two * rest)
        high, low = halves(total)
        sol_ref[own(s), :LANES] = high
        sol_ref[own(s), LANES:] = low

    for level, body in enumerate((begin, sweep, residue, finish)):
        stage(level, body)

    lane_ids = lax.broadcasted_iota(jnp.int32, (GROUP, LANES), 1).astype(F32)
    for step in order:
        base = pl.multiple_of(to_group(step) * GROUP, GROUP)
        marks = labb_ref[pl.ds(base, GROUP), :] - 1.0
        chosen = jnp.concatenate(
            [hot(marks == lane_ids + float(k * LANES)) for k in range(nodal // LANES)], axis=1
        )
        back_ref[pl.ds(base, GROUP), :] = folded(dot(chosen, sol_ref[...]))
        send_group(back_ref, ret_ref, back_send, back_recv, step)

    slot_lanes = lax.broadcasted_iota(jnp.int32, (blocks, LANES), 1)
    for k, step in enumerate(order):
        group_copy(back_ref, ret_ref, back_send, back_recv, step).wait_recv()
        base = pl.multiple_of(from_group(step) * GROUP, GROUP)
        places = posb_ref[...].astype(jnp.int32) - base
        chosen = jnp.concatenate(
            [hot(places == slot_lanes), hot(places == slot_lanes + LANES)], axis=1
        )
        high, low = halves(ret_ref[pl.ds(base, GROUP), :])
        part = folded(dot(chosen, jnp.concatenate([high, low], axis=1)))
        acc_ref[...] = part if k == 0 else acc_ref[...] + part

    def lift(g, _):
        cols = pl.ds(pl.multiple_of(g * LANES, LANES), LANES)
        values = acc_ref[cols, :].T

        for k in range(BLOCK_EDGES // 8):
            rows = slice(k * 8, k * 8 + 8)

            def taken(c, ids, part):
                found = None
                for piece in range(NODE_BLOCK // 8):
                    start = c * NODE_BLOCK + piece * 8
                    here = jnp.take_along_axis(
                        values[start : start + 8], ids, axis=0, mode="promise_in_bounds"
                    )
                    found = here if piece == 0 else jnp.where(part == piece, here, found)
                return found

            tails = ends_ref[0, rows, cols]
            heads = ends_ref[1, rows, cols]
            tail_at, tail_part = tails & 7, tails >> 3
            head_at, head_part = heads & 7, heads >> 3
            total = None
            for c in range(3):
                pair = taken(c, head_at, head_part) + taken(c, tail_at, tail_part)
                term = tangent_ref[c, rows, cols] * pair
                total = term if c == 0 else total + term
            drop = taken(3, head_at, head_part) - taken(3, tail_at, tail_part)
            out_ref[rows, cols] = (
                jacobi_ref[rows, cols] * resid_ref[rows, cols] + 0.5 * total + drop
            )
        return 0

    lax.fori_loop(0, lane_groups, lift, 0)

    for step in order:
        group_copy(send_ref, got_ref, go_send, go_recv, step).wait_send()
        group_copy(back_ref, ret_ref, back_send, back_recv, step).wait_send()
    for level in range(3):
        for side in range(2):
            halo(level, side).wait_send()


def per_device(n, n_node, residual, tangent, jacobi, ends, target, node_block, sigma):
    blocks = residual.shape[1]
    slices, rows_radial, rows_axial = sigma.shape
    nodal = slices * rows_radial * rows_axial // NODE_BLOCK
    slab = nodal // slices
    slots = 2 * blocks
    width = 4 * NODE_BLOCK
    cells = sigma.reshape(nodal, NODE_BLOCK)
    diag = 6.0 + jnp.concatenate([cells, cells, cells, 0.5 * cells], axis=1)
    groups = slots // GROUP
    vmem = pl.BlockSpec(memory_space=pltpu.VMEM)
    return pl.pallas_call(
        functools.partial(kernel, n, n_node, slices, rows_radial),
        out_shape=jax.ShapeDtypeStruct(residual.shape, F32),
        in_specs=[vmem] * 7,
        out_specs=vmem,
        scratch_shapes=[
            pltpu.VMEM((1, blocks), jnp.int32),
            pltpu.VMEM((blocks, LANES), F32),
            pltpu.VMEM((n, 1, LANES), F32),
            pltpu.VMEM((n, 1, LANES), F32),
            pltpu.VMEM((slots, LANES), F32),
            pltpu.VMEM((blocks, 2 * width), BF16),
            pltpu.VMEM((slots, width), F32),
            pltpu.VMEM((slots, width), F32),
            pltpu.VMEM((nodal, width), F32),
            pltpu.VMEM((nodal, width), F32),
            pltpu.VMEM((3, nodal + 2 * slab, width), F32),
            pltpu.VMEM((nodal, 2 * width), BF16),
            pltpu.VMEM((slots, width), F32),
            pltpu.VMEM((slots, width), F32),
            pltpu.SemaphoreType.DMA,
            pltpu.SemaphoreType.DMA,
            pltpu.SemaphoreType.DMA((groups,)),
            pltpu.SemaphoreType.DMA((groups,)),
            pltpu.SemaphoreType.DMA((groups,)),
            pltpu.SemaphoreType.DMA((groups,)),
            pltpu.SemaphoreType.DMA((3, 2)),
            pltpu.SemaphoreType.DMA((3, 2)),
        ],
        compiler_params=pltpu.CompilerParams(
            collective_id=0, has_side_effects=True, vmem_limit_bytes=48 * 1024 * 1024
        ),
    )(
        residual,
        tangent,
        jacobi,
        ends,
        target.reshape(1, blocks),
        node_block.reshape(1, blocks),
        diag,
    )


def solution(mesh):
    in_specs = (
        P(None, ("edge", "node")),
        P(None, None, ("edge", "node")),
        P(None, ("edge", "node")),
        P(None, None, ("edge", "node")),
        P(("edge", "node"), None),
        P(("edge", "node")),
        P(("edge", "node"), None, None),
    )
    out_specs = P(None, ("edge", "node"))
    n_node = mesh.shape["node"]
    n = mesh.shape["edge"] * n_node
    return jax.shard_map(
        functools.partial(per_device, n, n_node),
        mesh=mesh,
        in_specs=in_specs,
        out_specs=out_specs,
        check_vma=False,
    )
```

```python
import functools

import jax
import jax.numpy as jnp
from jax import lax
from jax.experimental import pallas as pl
from jax.experimental.pallas import tpu as pltpu
from jax.sharding import PartitionSpec as P

BLOCK_EDGES = 64
NODE_BLOCK = 32
LANES = 128
GROUP = 256

F32 = jnp.float32
BF16 = jnp.bfloat16
MESH = pl.DeviceIdType.MESH


def halves(values):
    high = values.astype(BF16)
    low = (values - high.astype(F32)).astype(BF16)
    return high, low


def hot(mask):
    return jnp.where(mask, 1.0, 0.0).astype(BF16)


def dot(a, b):
    return jnp.dot(a, b, preferred_element_type=F32)


def folded(product):
    return product[:, :LANES] + product[:, LANES:]


def order_of(groups):
    return [(groups // 2 + 3 * k) % groups for k in range(groups)]


def kernel(
    n,
    n_node,
    slices,
    resid_ref,
    tangent_ref,
    jacobi_ref,
    ends_ref,
    target_ref,
    label_ref,
    diag_ref,
    out_ref,
    pos_ref,
    posb_ref,
    lab_out,
    lab_in,
    labb_ref,
    rows_ref,
    send_ref,
    got_ref,
    acc_ref,
    rest_ref,
    field_ref,
    sol_ref,
    back_ref,
    ret_ref,
    mine_ref,
    lab_send,
    lab_recv,
    go_send,
    go_recv,
    back_send,
    back_recv,
    halo_send,
    halo_recv,
):
    me = lax.axis_index("edge") * n_node + lax.axis_index("node")
    blocks = resid_ref.shape[1]
    lane_groups = blocks // LANES
    cap = 2 * blocks // n
    deep = cap // 2
    peers = GROUP // cap
    groups = n // peers
    my_group = me // peers
    my_place = lax.rem(me, peers)
    slab = LANES
    nodal = slices * slab
    order = order_of(groups)

    def device(t):
        return (t // n_node, lax.rem(t, n_node))

    def to_group(step):
        return lax.rem(my_group + step, groups)

    def from_group(step):
        return lax.rem(my_group + groups - step, groups)

    def partner(group, turn):
        return group * peers + lax.rem(my_place + turn, peers)

    barrier = pltpu.get_barrier_semaphore()
    for step in range(1, n):
        pl.semaphore_signal(
            barrier, inc=1, device_id=device(lax.rem(me + step, n)), device_id_type=MESH
        )

    upper = hot(
        lax.broadcasted_iota(jnp.int32, (LANES, LANES), 0)
        <= lax.broadcasted_iota(jnp.int32, (LANES, LANES), 1)
    )
    device_ids = lax.broadcasted_iota(jnp.int32, (n, LANES), 0)
    slot_ids = lax.broadcasted_iota(jnp.int32, (GROUP, LANES), 0)
    carry = jnp.zeros((n, 1), F32)
    label_sum = jnp.zeros((2 * n, GROUP), F32)
    offset = my_place * deep
    for g in range(lane_groups):
        cols = slice(g * LANES, (g + 1) * LANES)
        named = target_ref[:, cols]
        match = jnp.where(device_ids == named, 1.0, 0.0)
        local = dot(match.astype(BF16), upper)
        rank = jnp.sum(match * (local + carry), axis=0, keepdims=True) - 1.0
        carry = carry + local[:, LANES - 1 :]
        rank = rank.astype(jnp.int32)
        slot = jnp.where(rank < deep, rank, rank - deep + LANES)
        row = named * deep
        place = (row & (LANES - 1)) + 2 * (row - (row & (LANES - 1))) + slot
        pos_ref[:, cols] = place
        posb_ref[cols, :] = jnp.broadcast_to(place.astype(F32), (LANES, LANES)).T
        mark = label_ref[:, cols] + 1
        high = match * (mark >> 5).astype(F32)
        low = match * (mark & 31).astype(F32)
        label_sum = label_sum + lax.dot_general(
            jnp.concatenate([high, low], axis=0).astype(BF16),
            hot(slot_ids == slot + offset),
            (((1,), (1,)), ((), ())),
            preferred_element_type=F32,
        )
    labels = 32.0 * label_sum[:n] + label_sum[n:]
    for t in range(n):
        lab_out[t] = labels[t : t + 1]

    pl.semaphore_wait(barrier, n - 1)

    lab_in[me] = lab_out[me]
    for step in range(1, n):
        t = lax.rem(me + step, n)
        pltpu.make_async_remote_copy(
            src_ref=lab_out.at[t],
            dst_ref=lab_in.at[me],
            send_sem=lab_send,
            recv_sem=lab_recv,
            device_id=device(t),
            device_id_type=MESH,
        ).start()

    lane = lax.broadcasted_iota(jnp.int32, (1, LANES), 1)
    left_lanes = lane < LANES // 2

    def split(values):
        other = pltpu.roll(values, LANES // 2, 1)
        return (
            (jnp.where(left_lanes, values, 0.0), jnp.where(left_lanes, other, 0.0)),
            (jnp.where(left_lanes, 0.0, other), jnp.where(left_lanes, 0.0, values)),
        )

    node_ids = lax.broadcasted_iota(jnp.int32, (NODE_BLOCK, LANES), 0)

    def find_terms(half):
        def terms_of(g, _):
            cols = pl.ds(pl.multiple_of(g * LANES, LANES), LANES)

            def chunk(k, sums):
                rows = pl.ds(pl.multiple_of(k * 8, 8), 8)
                residual = resid_ref[rows, cols]
                halved = 0.5 * residual
                vectors = [
                    tangent_ref[c, rows, cols] * halved for c in range(2 * half, min(3, 2 * half + 2))
                ]
                tails = ends_ref[0, rows, cols]
                heads = ends_ref[1, rows, cols]
                sums = list(sums)
                for e in range(8):
                    at_tail = node_ids == tails[e : e + 1]
                    at_head = node_ids == heads[e : e + 1]
                    either = at_tail | at_head
                    for c, vector in enumerate(vectors):
                        sums[c] = sums[c] + jnp.where(either, vector[e : e + 1], 0.0)
                    if half:
                        value = residual[e : e + 1]
                        sums[1] = sums[1] + jnp.where(
                            at_head, value, jnp.where(at_tail, -value, 0.0)
                        )
                return tuple(sums)

            zero = jnp.zeros((NODE_BLOCK, LANES), F32)
            sums = lax.fori_loop(0, BLOCK_EDGES // 8, chunk, (zero,) * 2)
            turned = jnp.concatenate(list(sums) + [zero, zero], axis=0).T
            for side, values in enumerate((turned, pltpu.roll(turned, LANES // 2, 1))):
                at = pl.ds(pl.multiple_of(side * blocks + g * LANES, LANES), LANES)
                high, low = halves(values)
                rows_ref[half, at, :LANES] = high
                rows_ref[half, at, LANES:] = low
            return 0

        lax.fori_loop(0, lane_groups, terms_of, 0)

    def rows_copy(src, dst, sends, recvs, half, step, turn):
        t = partner(to_group(step), turn)
        return pltpu.make_async_remote_copy(
            src_ref=src.at[half, pl.ds(pl.multiple_of(t * deep, deep), deep)],
            dst_ref=dst.at[half, pl.ds(pl.multiple_of(me * deep, deep), deep)],
            send_sem=sends.at[half, step],
            recv_sem=recvs.at[half, step],
            device_id=device(t),
            device_id_type=MESH,
        )

    def group_copy(src, dst, sends, recvs, half, step):
        size = LANES if step else LANES - deep
        return pltpu.make_async_remote_copy(
            src_ref=src.at[half, pl.ds(0, size)],
            dst_ref=dst.at[half, pl.ds(0, size)],
            send_sem=sends.at[half, step],
            recv_sem=recvs.at[half, step],
            device_id=device(me),
            device_id_type=MESH,
        )

    def send_group(src, dst, sends, recvs, half, step):
        for turn in range(peers):
            if step == 0 and turn == 0:
                mine = pl.ds(pl.multiple_of(me * deep, deep), deep)
                dst[half, mine, :] = src[half, mine, :]
            else:
                rows_copy(src, dst, sends, recvs, half, step, turn).start()

    row_ids = lax.broadcasted_iota(jnp.int32, (LANES, blocks), 0)

    def send_terms(half):
        for step in order:
            group = to_group(step)
            places = pos_ref[...] - group * GROUP
            chosen = jnp.concatenate(
                [hot(places == row_ids), hot(places == row_ids + LANES)], axis=1
            )
            at = pl.ds(pl.multiple_of(group * LANES, LANES), LANES)
            send_ref[half, at, :] = folded(dot(chosen, rows_ref[half]))
            send_group(send_ref, got_ref, go_send, go_recv, half, step)

    def label_row(group):
        total = lab_in[group * peers]
        for k in range(1, peers):
            total = total + lab_in[group * peers + k]
        return total

    def take_labels():
        pltpu.make_async_remote_copy(
            src_ref=lab_out.at[pl.ds(0, n - 1)],
            dst_ref=lab_in.at[pl.ds(0, n - 1)],
            send_sem=lab_send,
            recv_sem=lab_recv,
            device_id=device(me),
            device_id_type=MESH,
        ).wait()
        for g in range(groups):
            row = label_row(g)
            for k in range(2):
                at = slice(g * GROUP + k * LANES, g * GROUP + (k + 1) * LANES)
                labb_ref[at, :] = jnp.broadcast_to(
                    row[:, k * LANES : (k + 1) * LANES], (LANES, LANES)
                ).T

    def block_ids(side):
        rows = lax.broadcasted_iota(jnp.int32, (slab, LANES), 0)
        return jnp.concatenate(
            [(rows + (2 * s + side) * slab + 1).astype(F32) for s in range(slices)], axis=0
        )

    def sum_terms(half):
        for k, step in enumerate(order):
            group_copy(send_ref, got_ref, go_send, go_recv, half, step).wait_recv()
            source = from_group(step)
            marks = label_row(source)
            chosen = jnp.concatenate(
                [
                    hot(block_ids(side) == marks[:, part * LANES : (part + 1) * LANES])
                    for side in range(2)
                    for part in range(2)
                ],
                axis=1,
            )
            got = got_ref[half, pl.ds(pl.multiple_of(source * LANES, LANES), LANES), :]
            placed = split(got)
            high, low = halves(jnp.concatenate(placed[0] + placed[1], axis=0))
            part = folded(dot(chosen, jnp.concatenate([high, low], axis=1)))
            acc_ref[half] = part if k == 0 else acc_ref[half] + part

    inner = lax.broadcasted_iota(jnp.int32, (slab, LANES), 0) & 7
    node = lax.broadcasted_iota(jnp.int32, (slab, LANES), 1) & (NODE_BLOCK - 1)
    last_node = node == NODE_BLOCK - 1
    first_node = node == 0
    last_inner = inner == 7
    first_inner = inner == 0
    left = lax.rem(me + n - 1, n)
    right = lax.rem(me + 1, n)

    def own(s):
        return slice(s * slab, (s + 1) * slab)

    def stored(s):
        return slice((s + 1) * slab, (s + 2) * slab)

    def halo(half, level, side):
        at = stored(0) if side == 0 else stored(slices - 1)
        to = stored(slices) if side == 0 else own(0)
        return pltpu.make_async_remote_copy(
            src_ref=field_ref.at[half, level, at],
            dst_ref=field_ref.at[half, level, to],
            send_sem=halo_send.at[half, level, side],
            recv_sem=halo_recv.at[half, level, side],
            device_id=device(left if side == 0 else right),
            device_id_type=MESH,
        )

    def smooth(half):
        scale = jnp.where((lane & (LANES // 2 - 1)) < NODE_BLOCK, 1.0, 0.5 if half else 1.0)
        scale = scale.astype(F32)
        top = 12.0 + 8.0 * scale
        bottom = top / 8.0
        centre = (top + bottom) / 2.0
        radius = (top - bottom) / 2.0
        ratio = centre / radius
        first = 1.0 / ratio
        second = 1.0 / (2.0 * ratio - first)
        coef_one = second * first
        coef_two = 2.0 * second / radius
        inverse = 1.0 / centre

        def applied(level, s):
            field = field_ref.at[half, level]
            here = field[stored(s)]
            beside = field[own(s)] + field[stored(s + 1)]
            inward = jnp.where(left_lanes, 0.0, pltpu.roll(here[-8:], LANES // 2, 1))
            outward = jnp.where(left_lanes, pltpu.roll(here[:8], LANES // 2, 1), 0.0)
            beside = beside + jnp.concatenate([inward, here[:-8]], axis=0)
            beside = beside + jnp.concatenate([here[8:], outward], axis=0)
            after = pltpu.roll(pltpu.roll(here, slab - 1, 0), NODE_BLOCK - 1, 1)
            after = jnp.where(last_inner, 0.0, after)
            before = pltpu.roll(pltpu.roll(here, 1, 0), LANES - NODE_BLOCK + 1, 1)
            before = jnp.where(first_inner, 0.0, before)
            beside = beside + jnp.where(last_node, after, pltpu.roll(here, LANES - 1, 1))
            beside = beside + jnp.where(first_node, before, pltpu.roll(here, 1, 1))
            return diag_ref[half, own(s)] * here - beside

        def stage(level, body):
            if level:
                for side in range(2):
                    halo(half, level - 1, side).wait_recv()
            for s in (0, slices - 1):
                body(s)
            if level < 3:
                for side in range(2):
                    halo(half, level, side).start()
            for s in range(1, slices - 1):
                body(s)

        def begin(s):
            field_ref[half, 0, stored(s)] = acc_ref[half, own(s)] * inverse

        def sweep(s):
            rest = acc_ref[half, own(s)] - applied(0, s)
            step = field_ref[half, 0, stored(s)]
            field_ref[half, 1, stored(s)] = step + (coef_one * step + coef_two * rest)

        def residue(s):
            rest = acc_ref[half, own(s)] - applied(1, s)
            rest_ref[half, own(s)] = rest
            field_ref[half, 2, stored(s)] = rest * inverse

        def finish(s):
            step = field_ref[half, 2, stored(s)]
            rest = rest_ref[half, own(s)] - applied(2, s)
            total = (field_ref[half, 1, stored(s)] + step) + (coef_one * step + coef_two * rest)
            placed = split(total)
            for part in range(2):
                for side in range(2):
                    start = (2 * part + side) * nodal + s * slab
                    high, low = halves(placed[part][side])
                    sol_ref[half, start : start + slab, :LANES] = high
                    sol_ref[half, start : start + slab, LANES:] = low

        for level, body in enumerate((begin, sweep, residue, finish)):
            stage(level, body)

    lane_ids = lax.broadcasted_iota(jnp.int32, (LANES, LANES), 1).astype(F32)

    def send_back(half):
        for step in order:
            group = to_group(step)
            chosen = []
            for part in range(2):
                start = pl.multiple_of(group * GROUP + part * LANES, LANES)
                marks = labb_ref[pl.ds(start, LANES), :] - 1.0
                for side in range(2):
                    for s in range(slices):
                        chosen.append(hot(marks == lane_ids + float((2 * s + side) * slab)))
            at = pl.ds(pl.multiple_of(group * LANES, LANES), LANES)
            back_ref[half, at, :] = folded(dot(jnp.concatenate(chosen, axis=1), sol_ref[half]))
            send_group(back_ref, ret_ref, back_send, back_recv, half, step)

    slot_lanes = lax.broadcasted_iota(jnp.int32, (blocks, LANES), 1).astype(F32)

    def take_back(half):
        for k, step in enumerate(order):
            group_copy(back_ref, ret_ref, back_send, back_recv, half, step).wait_recv()
            source = from_group(step)
            places = posb_ref[...] - (source * GROUP).astype(F32)
            chosen = jnp.concatenate(
                [hot(places == slot_lanes), hot(places == slot_lanes + float(LANES))], axis=1
            )
            got = ret_ref[half, pl.ds(pl.multiple_of(source * LANES, LANES), LANES), :]
            high = got.astype(BF16).astype(F32)
            low = got - high
            turn = LANES // 2
            pieces = [
                jnp.where(left_lanes, high, pltpu.roll(low, turn, 1)),
                jnp.where(left_lanes, pltpu.roll(high, turn, 1), low),
            ]
            part = dot(chosen, jnp.concatenate(pieces, axis=0).astype(BF16))
            mine_ref[...] = part if k == 0 else mine_ref[...] + part

    def lift(half):
        def lift_group(g, _):
            cols = pl.ds(pl.multiple_of(g * LANES, LANES), LANES)
            values = mine_ref[cols, :].T
            values = values[: LANES // 2] + values[LANES // 2 :]

            for k in range(BLOCK_EDGES // 8):
                rows = slice(k * 8, k * 8 + 8)

                def taken(c, ids, part):
                    found = None
                    for piece in range(NODE_BLOCK // 8):
                        start = c * NODE_BLOCK + piece * 8
                        here = jnp.take_along_axis(
                            values[start : start + 8], ids, axis=0, mode="promise_in_bounds"
                        )
                        found = here if piece == 0 else jnp.where(part == piece, here, found)
                    return found

                tails = ends_ref[0, rows, cols]
                heads = ends_ref[1, rows, cols]
                tail_at, tail_part = tails & 7, tails >> 3
                head_at, head_part = heads & 7, heads >> 3
                pair = taken(0, head_at, head_part) + taken(0, tail_at, tail_part)
                total = tangent_ref[2 * half, rows, cols] * pair
                if half:
                    drop = taken(1, head_at, head_part) - taken(1, tail_at, tail_part)
                    out_ref[rows, cols] = out_ref[rows, cols] + 0.5 * total + drop
                else:
                    pair = taken(1, head_at, head_part) + taken(1, tail_at, tail_part)
                    total = total + tangent_ref[1, rows, cols] * pair
                    out_ref[rows, cols] = (
                        jacobi_ref[rows, cols] * resid_ref[rows, cols] + 0.5 * total
                    )
            return 0

        lax.fori_loop(0, lane_groups, lift_group, 0)

    for half in range(2):
        find_terms(half)
        send_terms(half)
    take_labels()
    for half in range(2):
        sum_terms(half)
        smooth(half)
        send_back(half)
    for half in range(2):
        take_back(half)
        lift(half)

    for half in range(2):
        for step in order:
            group_copy(send_ref, got_ref, go_send, go_recv, half, step).wait_send()
            group_copy(back_ref, ret_ref, back_send, back_recv, half, step).wait_send()
        for level in range(3):
            for side in range(2):
                halo(half, level, side).wait_send()


def per_device(n, n_node, residual, tangent, jacobi, ends, target, node_block, sigma):
    blocks = residual.shape[1]
    slices, rows_radial, rows_axial = sigma.shape
    nodal = slices * rows_radial * rows_axial // NODE_BLOCK // 2
    slots = 2 * blocks
    rows = slots // 2
    parts = sigma.reshape(slices, 2, LANES, NODE_BLOCK)
    inner, outer = (parts[:, k].reshape(nodal, NODE_BLOCK) for k in range(2))
    diag = 6.0 + jnp.stack(
        [
            jnp.concatenate([inner, inner, outer, outer], axis=1),
            jnp.concatenate([inner, 0.5 * inner, outer, 0.5 * outer], axis=1),
        ]
    )
    groups = slots // GROUP
    vmem = pl.BlockSpec(memory_space=pltpu.VMEM)
    return pl.pallas_call(
        functools.partial(kernel, n, n_node, slices),
        out_shape=jax.ShapeDtypeStruct(residual.shape, F32),
        in_specs=[vmem] * 7,
        out_specs=vmem,
        scratch_shapes=[
            pltpu.VMEM((1, blocks), jnp.int32),
            pltpu.VMEM((blocks, LANES), F32),
            pltpu.VMEM((n, 1, GROUP), F32),
            pltpu.VMEM((n, 1, GROUP), F32),
            pltpu.VMEM((slots, LANES), F32),
            pltpu.VMEM((2, 2 * blocks, 2 * LANES), BF16),
            pltpu.VMEM((2, rows, LANES), F32),
            pltpu.VMEM((2, rows, LANES), F32),
            pltpu.VMEM((2, nodal, LANES), F32),
            pltpu.VMEM((2, nodal, LANES), F32),
            pltpu.VMEM((2, 3, nodal + 2 * LANES, LANES), F32),
            pltpu.VMEM((2, 4 * nodal, 2 * LANES), BF16),
            pltpu.VMEM((2, rows, LANES), F32),
            pltpu.VMEM((2, rows, LANES), F32),
            pltpu.VMEM((blocks, LANES), F32),
            pltpu.SemaphoreType.DMA,
            pltpu.SemaphoreType.DMA,
            pltpu.SemaphoreType.DMA((2, groups)),
            pltpu.SemaphoreType.DMA((2, groups)),
            pltpu.SemaphoreType.DMA((2, groups)),
            pltpu.SemaphoreType.DMA((2, groups)),
            pltpu.SemaphoreType.DMA((2, 3, 2)),
            pltpu.SemaphoreType.DMA((2, 3, 2)),
        ],
        compiler_params=pltpu.CompilerParams(
            collective_id=0, has_side_effects=True, vmem_limit_bytes=48 * 1024 * 1024
        ),
    )(
        residual,
        tangent,
        jacobi,
        ends,
        target.reshape(1, blocks),
        node_block.reshape(1, blocks),
        diag,
    )


def solution(mesh):
    in_specs = (
        P(None, ("edge", "node")),
        P(None, None, ("edge", "node")),
        P(None, ("edge", "node")),
        P(None, None, ("edge", "node")),
        P(("edge", "node"), None),
        P(("edge", "node")),
        P(("edge", "node"), None, None),
    )
    out_specs = P(None, ("edge", "node"))
    n_node = mesh.shape["node"]
    n = mesh.shape["edge"] * n_node
    return jax.shard_map(
        functools.partial(per_device, n, n_node),
        mesh=mesh,
        in_specs=in_specs,
        out_specs=out_specs,
        check_vma=False,
    )
```

```python
import functools

import jax
import jax.numpy as jnp
from jax import lax
from jax.experimental import pallas as pl
from jax.experimental.pallas import tpu as pltpu
from jax.sharding import PartitionSpec as P

BLOCK_EDGES = 64
NODE_BLOCK = 32
LANES = 128
GROUP = 256

F32 = jnp.float32
BF16 = jnp.bfloat16
MESH = pl.DeviceIdType.MESH


def hot(mask):
    return jnp.where(mask, 1.0, 0.0).astype(BF16)


def dot(a, b):
    return jnp.dot(a, b, preferred_element_type=F32)


def left_lanes():
    return lax.broadcasted_iota(jnp.int32, (1, LANES), 1) < LANES // 2


def pieces(values):
    high = values.astype(BF16).astype(F32)
    low = values - high
    turn = LANES // 2
    upper = jnp.where(left_lanes(), high, pltpu.roll(low, turn, 1))
    lower = jnp.where(left_lanes(), pltpu.roll(high, turn, 1), low)
    return jnp.concatenate([upper, lower], axis=0).astype(BF16)


def folded(product):
    both = product + pltpu.roll(product, LANES // 2, 1)
    rows = product.shape[0] // 2
    return jnp.where(left_lanes(), both[:rows], both[rows:])


def order_of(groups):
    return [(groups // 2 + 3 * k) % groups for k in range(groups)]


def kernel(
    n,
    n_node,
    slices,
    resid_ref,
    tangent_ref,
    jacobi_ref,
    ends_ref,
    target_ref,
    label_ref,
    sigma_ref,
    out_ref,
    pos_ref,
    posb_ref,
    lab_out,
    lab_in,
    to_slot_ref,
    to_node_ref,
    from_node_ref,
    from_slot_ref,
    rows_ref,
    send_ref,
    got_ref,
    acc_ref,
    source_ref,
    wide_sigma_ref,
    first_ref,
    rest_ref,
    sol_ref,
    back_ref,
    ret_ref,
    mine_ref,
    lab_send,
    lab_recv,
    go_send,
    go_recv,
    back_send,
    back_recv,
    halo_send,
    halo_recv,
    sigma_send,
    sigma_recv,
):
    me = lax.axis_index("edge") * n_node + lax.axis_index("node")
    blocks = resid_ref.shape[1]
    lane_groups = blocks // LANES
    cap = 2 * blocks // n
    deep = cap // 2
    peers = GROUP // cap
    groups = n // peers
    my_group = me // peers
    my_place = lax.rem(me, peers)
    slab = LANES
    nodal = slices * slab
    order = order_of(groups)

    def device(t):
        return (t // n_node, lax.rem(t, n_node))

    def to_group(step):
        return lax.rem(my_group + step, groups)

    def from_group(step):
        return lax.rem(my_group + groups - step, groups)

    def partner(group, turn):
        return group * peers + lax.rem(my_place + turn, peers)

    barrier = pltpu.get_barrier_semaphore()
    for step in range(1, n):
        pl.semaphore_signal(
            barrier, inc=1, device_id=device(lax.rem(me + step, n)), device_id_type=MESH
        )

    upper = hot(
        lax.broadcasted_iota(jnp.int32, (LANES, LANES), 0)
        <= lax.broadcasted_iota(jnp.int32, (LANES, LANES), 1)
    )
    device_ids = lax.broadcasted_iota(jnp.int32, (n, LANES), 0)
    slot_ids = lax.broadcasted_iota(jnp.int32, (GROUP, LANES), 0)
    carry = jnp.zeros((n, 1), F32)
    label_sum = jnp.zeros((2 * n, GROUP), F32)
    offset = my_place * deep
    for g in range(lane_groups):
        cols = slice(g * LANES, (g + 1) * LANES)
        named = target_ref[:, cols]
        match = jnp.where(device_ids == named, 1.0, 0.0)
        local = dot(match.astype(BF16), upper)
        rank = jnp.sum(match * (local + carry), axis=0, keepdims=True) - 1.0
        carry = carry + local[:, LANES - 1 :]
        rank = rank.astype(jnp.int32)
        slot = jnp.where(rank < deep, rank, rank - deep + LANES)
        row = named * deep
        place = (row & (LANES - 1)) + 2 * (row - (row & (LANES - 1))) + slot
        pos_ref[:, cols] = place
        posb_ref[cols, :] = jnp.broadcast_to(place.astype(F32), (LANES, LANES)).T
        mark = label_ref[:, cols] + 1
        high = match * (mark >> 5).astype(F32)
        low = match * (mark & 31).astype(F32)
        label_sum = label_sum + lax.dot_general(
            jnp.concatenate([high, low], axis=0).astype(BF16),
            hot(slot_ids == slot + offset),
            (((1,), (1,)), ((), ())),
            preferred_element_type=F32,
        )
    labels = 32.0 * label_sum[:n] + label_sum[n:]
    for t in range(n):
        lab_out[t] = labels[t : t + 1]

    def send_labels():
        lab_in[me] = lab_out[me]
        for step in range(1, n):
            t = lax.rem(me + step, n)
            pltpu.make_async_remote_copy(
                src_ref=lab_out.at[t],
                dst_ref=lab_in.at[me],
                send_sem=lab_send,
                recv_sem=lab_recv,
                device_id=device(t),
                device_id_type=MESH,
            ).start()

    node_ids = lax.broadcasted_iota(jnp.int32, (NODE_BLOCK, LANES), 0)

    def find_terms(half):
        def terms_of(g, _):
            cols = pl.ds(pl.multiple_of(g * LANES, LANES), LANES)

            def chunk(k, sums):
                rows = pl.ds(pl.multiple_of(k * 8, 8), 8)
                residual = resid_ref[rows, cols]
                halved = 0.5 * residual
                vectors = [
                    tangent_ref[c, rows, cols] * halved for c in range(2 * half, min(3, 2 * half + 2))
                ]
                tails = ends_ref[0, rows, cols]
                heads = ends_ref[1, rows, cols]
                sums = list(sums)
                for e in range(8):
                    at_tail = node_ids == tails[e : e + 1]
                    at_head = node_ids == heads[e : e + 1]
                    either = at_tail | at_head
                    for c, vector in enumerate(vectors):
                        sums[c] = sums[c] + jnp.where(either, vector[e : e + 1], 0.0)
                    if half:
                        value = residual[e : e + 1]
                        sums[1] = sums[1] + jnp.where(
                            at_head, value, jnp.where(at_tail, -value, 0.0)
                        )
                return tuple(sums)

            zero = jnp.zeros((NODE_BLOCK, LANES), F32)
            sums = lax.fori_loop(0, BLOCK_EDGES // 8, chunk, (zero,) * 2)
            high = [total.astype(BF16).astype(F32) for total in sums]
            low = [total - part for total, part in zip(sums, high)]
            rows_ref[half, cols, :] = jnp.concatenate(high + low, axis=0).T.astype(BF16)
            return 0

        lax.fori_loop(0, lane_groups, terms_of, 0)

    def rows_copy(src, dst, sends, recvs, half, step, turn):
        t = partner(to_group(step), turn)
        return pltpu.make_async_remote_copy(
            src_ref=src.at[half, pl.ds(pl.multiple_of(t * deep, deep), deep)],
            dst_ref=dst.at[half, pl.ds(pl.multiple_of(me * deep, deep), deep)],
            send_sem=sends.at[half, step],
            recv_sem=recvs.at[half, step],
            device_id=device(t),
            device_id_type=MESH,
        )

    def group_copy(src, dst, sends, recvs, half, step):
        size = LANES if step else LANES - deep
        return pltpu.make_async_remote_copy(
            src_ref=src.at[half, pl.ds(0, size)],
            dst_ref=dst.at[half, pl.ds(0, size)],
            send_sem=sends.at[half, step],
            recv_sem=recvs.at[half, step],
            device_id=device(me),
            device_id_type=MESH,
        )

    def send_group(src, dst, sends, recvs, half, step):
        for turn in range(peers):
            if step == 0 and turn == 0:
                mine = pl.ds(pl.multiple_of(me * deep, deep), deep)
                dst[half, mine, :] = src[half, mine, :]
            else:
                rows_copy(src, dst, sends, recvs, half, step, turn).start()

    row_ids = lax.broadcasted_iota(jnp.int32, (GROUP, blocks), 0)

    def send_terms(half):
        for step in order:
            group = to_group(step)
            at = pl.ds(pl.multiple_of(group * GROUP, GROUP), GROUP)
            if half == 0:
                chosen = hot(pos_ref[...] - group * GROUP == row_ids)
                to_slot_ref[at, :] = chosen
            else:
                chosen = to_slot_ref[at, :]
            rows = pl.ds(pl.multiple_of(group * LANES, LANES), LANES)
            send_ref[half, rows, :] = folded(dot(chosen, rows_ref[half]))
            send_group(send_ref, got_ref, go_send, go_recv, half, step)

    slot_lanes = lax.broadcasted_iota(jnp.int32, (blocks, LANES), 1).astype(F32)

    def prepare_return():
        for g in range(groups):
            for part in range(2):
                lanes = slice(part * LANES, (part + 1) * LANES)
                ids = slot_lanes + float(g * GROUP + part * LANES)
                from_slot_ref[g, :, lanes] = hot(posb_ref[...] == ids)

    def label_row(group):
        total = lab_in[group * peers]
        for k in range(1, peers):
            total = total + lab_in[group * peers + k]
        return total

    def take_labels():
        pltpu.make_async_remote_copy(
            src_ref=lab_out.at[pl.ds(0, n - 1)],
            dst_ref=lab_in.at[pl.ds(0, n - 1)],
            send_sem=lab_send,
            recv_sem=lab_recv,
            device_id=device(me),
            device_id_type=MESH,
        ).wait()
        for g in range(groups):
            row = label_row(g)
            for part in range(2):
                lanes = slice(part * LANES, (part + 1) * LANES)
                marks = row[:, lanes]
                for side in range(2):
                    rows = slice(side * nodal, (side + 1) * nodal)
                    to_node_ref[g, rows, lanes] = hot(block_ids(side) == marks)
        for g in range(groups):
            row = label_row(g)
            for part in range(2):
                start = g * GROUP + part * LANES
                marks = row[:, part * LANES : (part + 1) * LANES]
                marks = jnp.broadcast_to(marks, (LANES, LANES)).T
                for side in range(2):
                    for s in range(slices):
                        column = side * nodal + s * slab
                        from_node_ref[start : start + LANES, column : column + slab] = hot(
                            marks == lane_ids + float((2 * s + side) * slab + 1)
                        )

    def block_ids(side):
        rows = lax.broadcasted_iota(jnp.int32, (slab, LANES), 0)
        return jnp.concatenate(
            [(rows + (2 * s + side) * slab + 1).astype(F32) for s in range(slices)], axis=0
        )

    lane_ids = lax.broadcasted_iota(jnp.int32, (LANES, LANES), 1).astype(F32)

    def sum_terms(half):
        for k, step in enumerate(order):
            group_copy(send_ref, got_ref, go_send, go_recv, half, step).wait_recv()
            source = from_group(step)
            got = got_ref[half, pl.ds(pl.multiple_of(source * LANES, LANES), LANES), :]
            part = dot(to_node_ref[source], pieces(got))
            acc_ref[...] = part if k == 0 else acc_ref[...] + part
        source_ref[half, at_slices(0, slices, 3)] = folded(acc_ref[...])

    inner = lax.broadcasted_iota(jnp.int32, (slab, LANES), 0) & 7
    node = lax.broadcasted_iota(jnp.int32, (slab, LANES), 1) & (NODE_BLOCK - 1)
    last_node = node == NODE_BLOCK - 1
    first_node = node == 0
    last_inner = inner == 7
    first_inner = inner == 0
    left = lax.rem(me + n - 1, n)
    right = lax.rem(me + 1, n)

    def at_slices(first, last, margin):
        return slice((first + margin) * slab, (last + margin) * slab)

    def halo(half, side):
        at = at_slices(0, 3, 3) if side == 0 else at_slices(slices - 3, slices, 3)
        to = at_slices(slices, slices + 3, 3) if side == 0 else at_slices(-3, 0, 3)
        return pltpu.make_async_remote_copy(
            src_ref=source_ref.at[half, at],
            dst_ref=source_ref.at[half, to],
            send_sem=halo_send.at[half, side],
            recv_sem=halo_recv.at[half, side],
            device_id=device(left if side == 0 else right),
            device_id_type=MESH,
        )

    def sigma_halo(side):
        at = at_slices(0, 2, 2) if side == 0 else at_slices(slices - 2, slices, 2)
        to = at_slices(slices, slices + 2, 2) if side == 0 else at_slices(-2, 0, 2)
        return pltpu.make_async_remote_copy(
            src_ref=wide_sigma_ref.at[at],
            dst_ref=wide_sigma_ref.at[to],
            send_sem=sigma_send.at[side],
            recv_sem=sigma_recv.at[side],
            device_id=device(left if side == 0 else right),
            device_id_type=MESH,
        )

    def smooth(half):
        lane = lax.broadcasted_iota(jnp.int32, (1, LANES), 1)
        scale = jnp.where((lane & (LANES // 2 - 1)) < NODE_BLOCK, 1.0, 0.5 if half else 1.0)
        scale = scale.astype(F32)
        top = 12.0 + 8.0 * scale
        bottom = top / 8.0
        centre = (top + bottom) / 2.0
        radius = (top - bottom) / 2.0
        ratio = centre / radius
        first = 1.0 / ratio
        second = 1.0 / (2.0 * ratio - first)
        coef_one = second * first
        coef_two = 2.0 * second / radius
        inverse = 1.0 / centre
        source = source_ref.at[half]

        def applied(field, margin, s):
            here = field[at_slices(s, s + 1, margin)]
            beside = field[at_slices(s - 1, s, margin)] + field[at_slices(s + 1, s + 2, margin)]
            turn = LANES // 2
            inward = jnp.where(left_lanes(), 0.0, pltpu.roll(here[-8:], turn, 1))
            outward = jnp.where(left_lanes(), pltpu.roll(here[:8], turn, 1), 0.0)
            beside = beside + jnp.concatenate([inward, here[:-8]], axis=0)
            beside = beside + jnp.concatenate([here[8:], outward], axis=0)
            after = pltpu.roll(pltpu.roll(here, slab - 1, 0), NODE_BLOCK - 1, 1)
            after = jnp.where(last_inner, 0.0, after)
            before = pltpu.roll(pltpu.roll(here, 1, 0), LANES - NODE_BLOCK + 1, 1)
            before = jnp.where(first_inner, 0.0, before)
            beside = beside + jnp.where(last_node, after, pltpu.roll(here, LANES - 1, 1))
            beside = beside + jnp.where(first_node, before, pltpu.roll(here, 1, 1))
            diag = 6.0 + scale * wide_sigma_ref[at_slices(s, s + 1, 2)]
            return here, diag * here - beside

        def sweep(s):
            here, image = applied(source, 3, s)
            step = here * inverse
            first_ref[at_slices(s, s + 1, 2)] = step + (
                coef_one * step + coef_two * (here - image * inverse)
            )

        def residue(s):
            image = applied(first_ref, 2, s)[1]
            rest_ref[at_slices(s, s + 1, 1)] = source[at_slices(s, s + 1, 3)] - image

        def finish(s):
            here, image = applied(rest_ref, 1, s)
            step = here * inverse
            total = (first_ref[at_slices(s, s + 1, 2)] + step) + (
                coef_one * step + coef_two * (here - image * inverse)
            )
            parts = pieces(total)
            for side in range(2):
                start = side * nodal + s * slab
                sol_ref[half, start : start + slab, :] = parts[side * slab : (side + 1) * slab]

        for side in range(2):
            halo(half, side).start()
        for s in range(1, slices - 1):
            sweep(s)
        for side in range(2):
            halo(half, side).wait_recv()
            if half == 0:
                sigma_halo(side).wait_recv()
        for s in [-2, -1, 0, slices - 1, slices, slices + 1]:
            sweep(s)
        for s in range(-1, slices + 1):
            residue(s)
        for s in range(slices):
            finish(s)

    def send_back(half):
        for step in order:
            group = to_group(step)
            chosen = from_node_ref[pl.ds(pl.multiple_of(group * GROUP, GROUP), GROUP), :]
            rows = pl.ds(pl.multiple_of(group * LANES, LANES), LANES)
            back_ref[half, rows, :] = folded(dot(chosen, sol_ref[half]))
            send_group(back_ref, ret_ref, back_send, back_recv, half, step)

    def take_back(half):
        for k, step in enumerate(order):
            group_copy(back_ref, ret_ref, back_send, back_recv, half, step).wait_recv()
            source = from_group(step)
            got = ret_ref[half, pl.ds(pl.multiple_of(source * LANES, LANES), LANES), :]
            part = dot(from_slot_ref[source], pieces(got))
            mine_ref[...] = part if k == 0 else mine_ref[...] + part

    def lift(half):
        def lift_group(g, _):
            cols = pl.ds(pl.multiple_of(g * LANES, LANES), LANES)
            values = mine_ref[cols, :].T
            values = values[: LANES // 2] + values[LANES // 2 :]

            for k in range(BLOCK_EDGES // 8):
                rows = slice(k * 8, k * 8 + 8)

                def taken(c, ids, part):
                    found = None
                    for piece in range(NODE_BLOCK // 8):
                        start = c * NODE_BLOCK + piece * 8
                        here = jnp.take_along_axis(
                            values[start : start + 8], ids, axis=0, mode="promise_in_bounds"
                        )
                        found = here if piece == 0 else jnp.where(part == piece, here, found)
                    return found

                tails = ends_ref[0, rows, cols]
                heads = ends_ref[1, rows, cols]
                tail_at, tail_part = tails & 7, tails >> 3
                head_at, head_part = heads & 7, heads >> 3
                pair = taken(0, head_at, head_part) + taken(0, tail_at, tail_part)
                total = tangent_ref[2 * half, rows, cols] * pair
                if half:
                    drop = taken(1, head_at, head_part) - taken(1, tail_at, tail_part)
                    out_ref[rows, cols] = out_ref[rows, cols] + 0.5 * total + drop
                else:
                    pair = taken(1, head_at, head_part) + taken(1, tail_at, tail_part)
                    total = total + tangent_ref[1, rows, cols] * pair
                    out_ref[rows, cols] = (
                        jacobi_ref[rows, cols] * resid_ref[rows, cols] + 0.5 * total
                    )
            return 0

        lax.fori_loop(0, lane_groups, lift_group, 0)

    wide_sigma_ref[at_slices(0, slices, 2)] = sigma_ref[...]
    find_terms(0)
    pl.semaphore_wait(barrier, n - 1)
    send_labels()
    send_terms(0)
    for side in range(2):
        sigma_halo(side).start()
    find_terms(1)
    send_terms(1)
    prepare_return()
    take_labels()
    for half in range(2):
        sum_terms(half)
        smooth(half)
        send_back(half)
    for half in range(2):
        take_back(half)
        lift(half)

    for half in range(2):
        for step in order:
            group_copy(send_ref, got_ref, go_send, go_recv, half, step).wait_send()
            group_copy(back_ref, ret_ref, back_send, back_recv, half, step).wait_send()
        for side in range(2):
            halo(half, side).wait_send()
    for side in range(2):
        sigma_halo(side).wait_send()


def per_device(n, n_node, residual, tangent, jacobi, ends, target, node_block, sigma):
    blocks = residual.shape[1]
    slices, rows_radial, rows_axial = sigma.shape
    nodal = slices * rows_radial * rows_axial // NODE_BLOCK // 2
    slots = 2 * blocks
    rows = slots // 2
    parts = sigma.reshape(slices, 2, LANES, NODE_BLOCK)
    inner, outer = (parts[:, k].reshape(nodal, NODE_BLOCK) for k in range(2))
    cells = jnp.concatenate([inner, inner, outer, outer], axis=1)
    groups = slots // GROUP
    vmem = pl.BlockSpec(memory_space=pltpu.VMEM)
    return pl.pallas_call(
        functools.partial(kernel, n, n_node, slices),
        out_shape=jax.ShapeDtypeStruct(residual.shape, F32),
        in_specs=[vmem] * 7,
        out_specs=vmem,
        scratch_shapes=[
            pltpu.VMEM((1, blocks), jnp.int32),
            pltpu.VMEM((blocks, LANES), F32),
            pltpu.VMEM((n, 1, GROUP), F32),
            pltpu.VMEM((n, 1, GROUP), F32),
            pltpu.VMEM((slots, blocks), BF16),
            pltpu.VMEM((groups, 2 * nodal, GROUP), BF16),
            pltpu.VMEM((slots, 2 * nodal), BF16),
            pltpu.VMEM((groups, blocks, GROUP), BF16),
            pltpu.VMEM((2, blocks, LANES), BF16),
            pltpu.VMEM((2, rows, LANES), F32),
            pltpu.VMEM((2, rows, LANES), F32),
            pltpu.VMEM((2 * nodal, LANES), F32),
            pltpu.VMEM((2, nodal + 6 * LANES, LANES), F32),
            pltpu.VMEM((nodal + 4 * LANES, LANES), F32),
            pltpu.VMEM((nodal + 4 * LANES, LANES), F32),
            pltpu.VMEM((nodal + 2 * LANES, LANES), F32),
            pltpu.VMEM((2, 2 * nodal, LANES), BF16),
            pltpu.VMEM((2, rows, LANES), F32),
            pltpu.VMEM((2, rows, LANES), F32),
            pltpu.VMEM((blocks, LANES), F32),
            pltpu.SemaphoreType.DMA,
            pltpu.SemaphoreType.DMA,
            pltpu.SemaphoreType.DMA((2, groups)),
            pltpu.SemaphoreType.DMA((2, groups)),
            pltpu.SemaphoreType.DMA((2, groups)),
            pltpu.SemaphoreType.DMA((2, groups)),
            pltpu.SemaphoreType.DMA((2, 2)),
            pltpu.SemaphoreType.DMA((2, 2)),
            pltpu.SemaphoreType.DMA((2,)),
            pltpu.SemaphoreType.DMA((2,)),
        ],
        compiler_params=pltpu.CompilerParams(
            collective_id=0, has_side_effects=True, vmem_limit_bytes=48 * 1024 * 1024
        ),
    )(
        residual,
        tangent,
        jacobi,
        ends,
        target.reshape(1, blocks),
        node_block.reshape(1, blocks),
        cells,
    )


def solution(mesh):
    in_specs = (
        P(None, ("edge", "node")),
        P(None, None, ("edge", "node")),
        P(None, ("edge", "node")),
        P(None, None, ("edge", "node")),
        P(("edge", "node"), None),
        P(("edge", "node")),
        P(("edge", "node"), None, None),
    )
    out_specs = P(None, ("edge", "node"))
    n_node = mesh.shape["node"]
    n = mesh.shape["edge"] * n_node
    return jax.shard_map(
        functools.partial(per_device, n, n_node),
        mesh=mesh,
        in_specs=in_specs,
        out_specs=out_specs,
        check_vma=False,
    )
```

```python
import functools

import jax
import jax.numpy as jnp
from jax import lax
from jax.experimental import pallas as pl
from jax.experimental.pallas import tpu as pltpu
from jax.sharding import PartitionSpec as P

BLOCK_EDGES = 64
NODE_BLOCK = 32
LANES = 128
GROUP = 256

F32 = jnp.float32
BF16 = jnp.bfloat16
MESH = pl.DeviceIdType.MESH


def hot(mask):
    return jnp.where(mask, 1.0, 0.0).astype(BF16)


def dot(a, b):
    return jnp.dot(a, b, preferred_element_type=F32)


def left_lanes():
    return lax.broadcasted_iota(jnp.int32, (1, LANES), 1) < LANES // 2


def pieces(values):
    high = values.astype(BF16).astype(F32)
    low = values - high
    turn = LANES // 2
    upper = jnp.where(left_lanes(), high, pltpu.roll(low, turn, 1))
    lower = jnp.where(left_lanes(), pltpu.roll(high, turn, 1), low)
    return jnp.concatenate([upper, lower], axis=0).astype(BF16)


def folded(product):
    both = product + pltpu.roll(product, LANES // 2, 1)
    rows = product.shape[0] // 2
    return jnp.where(left_lanes(), both[:rows], both[rows:])


def order_of(groups):
    return [(groups // 2 + 3 * k) % groups for k in range(groups)]


def kernel(
    n,
    n_node,
    slices,
    resid_in,
    tangent_in,
    ends_in,
    target_ref,
    label_ref,
    sigma_ref,
    out_ref,
    resid_ref,
    tangent_ref,
    ends_ref,
    load_sem,
    pos_ref,
    posb_ref,
    lab_out,
    lab_in,
    to_slot_ref,
    to_node_ref,
    from_node_ref,
    from_slot_ref,
    rows_ref,
    send_ref,
    got_ref,
    acc_ref,
    source_ref,
    wide_sigma_ref,
    first_ref,
    rest_ref,
    sol_ref,
    back_ref,
    ret_ref,
    mine_ref,
    lab_send,
    lab_recv,
    go_send,
    go_recv,
    back_send,
    back_recv,
    halo_send,
    halo_recv,
    sigma_send,
    sigma_recv,
):
    me = lax.axis_index("edge") * n_node + lax.axis_index("node")
    blocks = resid_ref.shape[1]
    lane_groups = blocks // LANES
    cap = 2 * blocks // n
    deep = cap // 2
    peers = GROUP // cap
    groups = n // peers
    my_group = me // peers
    my_place = lax.rem(me, peers)
    slab = LANES
    nodal = slices * slab
    order = order_of(groups)

    def device(t):
        return (t // n_node, lax.rem(t, n_node))

    def to_group(step):
        return lax.rem(my_group + step, groups)

    def from_group(step):
        return lax.rem(my_group + groups - step, groups)

    def partner(group, turn):
        return group * peers + lax.rem(my_place + turn, peers)

    barrier = pltpu.get_barrier_semaphore()
    for step in range(1, n):
        pl.semaphore_signal(
            barrier, inc=1, device_id=device(lax.rem(me + step, n)), device_id_type=MESH
        )

    loads = [
        pltpu.make_async_copy(src, dst, load_sem.at[k])
        for k, (src, dst) in enumerate(
            ((resid_in, resid_ref), (ends_in, ends_ref), (tangent_in, tangent_ref))
        )
    ]
    for load in loads:
        load.start()

    upper = hot(
        lax.broadcasted_iota(jnp.int32, (LANES, LANES), 0)
        <= lax.broadcasted_iota(jnp.int32, (LANES, LANES), 1)
    )
    device_ids = lax.broadcasted_iota(jnp.int32, (n, LANES), 0)
    slot_ids = lax.broadcasted_iota(jnp.int32, (GROUP, LANES), 0)
    carry = jnp.zeros((n, 1), F32)
    label_sum = jnp.zeros((2 * n, GROUP), F32)
    offset = my_place * deep
    for g in range(lane_groups):
        cols = slice(g * LANES, (g + 1) * LANES)
        named = target_ref[:, cols]
        match = jnp.where(device_ids == named, 1.0, 0.0)
        local = dot(match.astype(BF16), upper)
        rank = jnp.sum(match * (local + carry), axis=0, keepdims=True) - 1.0
        carry = carry + local[:, LANES - 1 :]
        rank = rank.astype(jnp.int32)
        slot = jnp.where(rank < deep, rank, rank - deep + LANES)
        row = named * deep
        place = (row & (LANES - 1)) + 2 * (row - (row & (LANES - 1))) + slot
        pos_ref[:, cols] = place
        posb_ref[cols, :] = jnp.broadcast_to(place.astype(F32), (LANES, LANES)).T
        mark = label_ref[:, cols] + 1
        high = match * (mark >> 5).astype(F32)
        low = match * (mark & 31).astype(F32)
        label_sum = label_sum + lax.dot_general(
            jnp.concatenate([high, low], axis=0).astype(BF16),
            hot(slot_ids == slot + offset),
            (((1,), (1,)), ((), ())),
            preferred_element_type=F32,
        )
    labels = 32.0 * label_sum[:n] + label_sum[n:]
    for t in range(n):
        lab_out[t] = labels[t : t + 1]

    def send_labels():
        lab_in[me] = lab_out[me]
        for step in range(1, n):
            t = lax.rem(me + step, n)
            pltpu.make_async_remote_copy(
                src_ref=lab_out.at[t],
                dst_ref=lab_in.at[me],
                send_sem=lab_send,
                recv_sem=lab_recv,
                device_id=device(t),
                device_id_type=MESH,
            ).start()

    node_ids = lax.broadcasted_iota(jnp.int32, (NODE_BLOCK, LANES), 0)

    def find_terms(half):
        def terms_of(g, _):
            cols = pl.ds(pl.multiple_of(g * LANES, LANES), LANES)

            def chunk(k, sums):
                rows = pl.ds(pl.multiple_of(k * 8, 8), 8)
                residual = resid_ref[rows, cols]
                halved = 0.5 * residual
                vectors = [
                    tangent_ref[c, rows, cols] * halved for c in range(2 * half, min(3, 2 * half + 2))
                ]
                tails = ends_ref[0, rows, cols]
                heads = ends_ref[1, rows, cols]
                sums = list(sums)
                for e in range(8):
                    at_tail = node_ids == tails[e : e + 1]
                    at_head = node_ids == heads[e : e + 1]
                    either = at_tail | at_head
                    for c, vector in enumerate(vectors):
                        sums[c] = sums[c] + jnp.where(either, vector[e : e + 1], 0.0)
                    if half:
                        value = residual[e : e + 1]
                        sums[1] = sums[1] + jnp.where(
                            at_head, value, jnp.where(at_tail, -value, 0.0)
                        )
                return tuple(sums)

            zero = jnp.zeros((NODE_BLOCK, LANES), F32)
            sums = lax.fori_loop(0, BLOCK_EDGES // 8, chunk, (zero,) * 2)
            high = [total.astype(BF16).astype(F32) for total in sums]
            low = [total - part for total, part in zip(sums, high)]
            rows_ref[half, cols, :] = jnp.concatenate(high + low, axis=0).T.astype(BF16)
            return 0

        lax.fori_loop(0, lane_groups, terms_of, 0)

    def rows_copy(src, dst, sends, recvs, half, step, turn):
        t = partner(to_group(step), turn)
        return pltpu.make_async_remote_copy(
            src_ref=src.at[half, pl.ds(pl.multiple_of(t * deep, deep), deep)],
            dst_ref=dst.at[half, pl.ds(pl.multiple_of(me * deep, deep), deep)],
            send_sem=sends.at[half, step],
            recv_sem=recvs.at[half, step],
            device_id=device(t),
            device_id_type=MESH,
        )

    def group_copy(src, dst, sends, recvs, half, step):
        size = LANES if step else LANES - deep
        return pltpu.make_async_remote_copy(
            src_ref=src.at[half, pl.ds(0, size)],
            dst_ref=dst.at[half, pl.ds(0, size)],
            send_sem=sends.at[half, step],
            recv_sem=recvs.at[half, step],
            device_id=device(me),
            device_id_type=MESH,
        )

    def send_group(src, dst, sends, recvs, half, step):
        for turn in range(peers):
            if step == 0 and turn == 0:
                mine = pl.ds(pl.multiple_of(me * deep, deep), deep)
                dst[half, mine, :] = src[half, mine, :]
            else:
                rows_copy(src, dst, sends, recvs, half, step, turn).start()

    row_ids = lax.broadcasted_iota(jnp.int32, (GROUP, blocks), 0)

    def send_terms(half, steps):
        for step in steps:
            group = to_group(step)
            at = pl.ds(pl.multiple_of(group * GROUP, GROUP), GROUP)
            if half == 0:
                chosen = hot(pos_ref[...] - group * GROUP == row_ids)
                to_slot_ref[at, :] = chosen
            else:
                chosen = to_slot_ref[at, :]
            rows = pl.ds(pl.multiple_of(group * LANES, LANES), LANES)
            send_ref[half, rows, :] = folded(dot(chosen, rows_ref[half]))
            send_group(send_ref, got_ref, go_send, go_recv, half, step)

    slot_lanes = lax.broadcasted_iota(jnp.int32, (blocks, LANES), 1).astype(F32)

    def prepare_return():
        for g in range(groups):
            for part in range(2):
                lanes = slice(part * LANES, (part + 1) * LANES)
                ids = slot_lanes + float(g * GROUP + part * LANES)
                from_slot_ref[g, :, lanes] = hot(posb_ref[...] == ids)

    def label_row(group):
        total = lab_in[group * peers]
        for k in range(1, peers):
            total = total + lab_in[group * peers + k]
        return total

    def take_labels():
        pltpu.make_async_remote_copy(
            src_ref=lab_out.at[pl.ds(0, n - 1)],
            dst_ref=lab_in.at[pl.ds(0, n - 1)],
            send_sem=lab_send,
            recv_sem=lab_recv,
            device_id=device(me),
            device_id_type=MESH,
        ).wait()
        for g in range(groups):
            row = label_row(g)
            for part in range(2):
                lanes = slice(part * LANES, (part + 1) * LANES)
                marks = row[:, lanes]
                for side in range(2):
                    rows = slice(side * nodal, (side + 1) * nodal)
                    to_node_ref[g, rows, lanes] = hot(block_ids(side) == marks)
        for g in range(groups):
            row = label_row(g)
            for part in range(2):
                start = g * GROUP + part * LANES
                marks = row[:, part * LANES : (part + 1) * LANES]
                marks = jnp.broadcast_to(marks, (LANES, LANES)).T
                for side in range(2):
                    for s in range(slices):
                        column = side * nodal + s * slab
                        from_node_ref[start : start + LANES, column : column + slab] = hot(
                            marks == lane_ids + float((2 * s + side) * slab + 1)
                        )

    def block_ids(side):
        rows = lax.broadcasted_iota(jnp.int32, (slab, LANES), 0)
        return jnp.concatenate(
            [(rows + (2 * s + side) * slab + 1).astype(F32) for s in range(slices)], axis=0
        )

    lane_ids = lax.broadcasted_iota(jnp.int32, (LANES, LANES), 1).astype(F32)

    def sum_terms(half):
        for k, step in enumerate(order):
            group_copy(send_ref, got_ref, go_send, go_recv, half, step).wait_recv()
            source = from_group(step)
            got = got_ref[half, pl.ds(pl.multiple_of(source * LANES, LANES), LANES), :]
            part = dot(to_node_ref[source], pieces(got))
            acc_ref[...] = part if k == 0 else acc_ref[...] + part
        source_ref[half, at_slices(0, slices, 3)] = folded(acc_ref[...])

    inner = lax.broadcasted_iota(jnp.int32, (slab, LANES), 0) & 7
    node = lax.broadcasted_iota(jnp.int32, (slab, LANES), 1) & (NODE_BLOCK - 1)
    last_node = node == NODE_BLOCK - 1
    first_node = node == 0
    last_inner = inner == 7
    first_inner = inner == 0
    left = lax.rem(me + n - 1, n)
    right = lax.rem(me + 1, n)

    def at_slices(first, last, margin):
        return slice((first + margin) * slab, (last + margin) * slab)

    def halo(half, side):
        at = at_slices(0, 3, 3) if side == 0 else at_slices(slices - 3, slices, 3)
        to = at_slices(slices, slices + 3, 3) if side == 0 else at_slices(-3, 0, 3)
        return pltpu.make_async_remote_copy(
            src_ref=source_ref.at[half, at],
            dst_ref=source_ref.at[half, to],
            send_sem=halo_send.at[half, side],
            recv_sem=halo_recv.at[half, side],
            device_id=device(left if side == 0 else right),
            device_id_type=MESH,
        )

    def sigma_halo(side):
        at = at_slices(0, 2, 2) if side == 0 else at_slices(slices - 2, slices, 2)
        to = at_slices(slices, slices + 2, 2) if side == 0 else at_slices(-2, 0, 2)
        return pltpu.make_async_remote_copy(
            src_ref=wide_sigma_ref.at[at],
            dst_ref=wide_sigma_ref.at[to],
            send_sem=sigma_send.at[side],
            recv_sem=sigma_recv.at[side],
            device_id=device(left if side == 0 else right),
            device_id_type=MESH,
        )

    def smooth(half):
        lane = lax.broadcasted_iota(jnp.int32, (1, LANES), 1)
        scale = jnp.where((lane & (LANES // 2 - 1)) < NODE_BLOCK, 1.0, 0.5 if half else 1.0)
        scale = scale.astype(F32)
        top = 12.0 + 8.0 * scale
        bottom = top / 8.0
        centre = (top + bottom) / 2.0
        radius = (top - bottom) / 2.0
        ratio = centre / radius
        first = 1.0 / ratio
        second = 1.0 / (2.0 * ratio - first)
        coef_one = second * first
        coef_two = 2.0 * second / radius
        inverse = 1.0 / centre
        source = source_ref.at[half]

        def applied(field, margin, s):
            here = field[at_slices(s, s + 1, margin)]
            beside = field[at_slices(s - 1, s, margin)] + field[at_slices(s + 1, s + 2, margin)]
            turn = LANES // 2
            inward = jnp.where(left_lanes(), 0.0, pltpu.roll(here[-8:], turn, 1))
            outward = jnp.where(left_lanes(), pltpu.roll(here[:8], turn, 1), 0.0)
            beside = beside + jnp.concatenate([inward, here[:-8]], axis=0)
            beside = beside + jnp.concatenate([here[8:], outward], axis=0)
            after = pltpu.roll(pltpu.roll(here, slab - 1, 0), NODE_BLOCK - 1, 1)
            after = jnp.where(last_inner, 0.0, after)
            before = pltpu.roll(pltpu.roll(here, 1, 0), LANES - NODE_BLOCK + 1, 1)
            before = jnp.where(first_inner, 0.0, before)
            beside = beside + jnp.where(last_node, after, pltpu.roll(here, LANES - 1, 1))
            beside = beside + jnp.where(first_node, before, pltpu.roll(here, 1, 1))
            diag = 6.0 + scale * wide_sigma_ref[at_slices(s, s + 1, 2)]
            return here, diag * here - beside

        def sweep(s):
            here, image = applied(source, 3, s)
            step = here * inverse
            first_ref[at_slices(s, s + 1, 2)] = step + (
                coef_one * step + coef_two * (here - image * inverse)
            )

        def residue(s):
            image = applied(first_ref, 2, s)[1]
            rest_ref[at_slices(s, s + 1, 1)] = source[at_slices(s, s + 1, 3)] - image

        def finish(s):
            here, image = applied(rest_ref, 1, s)
            step = here * inverse
            total = (first_ref[at_slices(s, s + 1, 2)] + step) + (
                coef_one * step + coef_two * (here - image * inverse)
            )
            parts = pieces(total)
            for side in range(2):
                start = side * nodal + s * slab
                sol_ref[half, start : start + slab, :] = parts[side * slab : (side + 1) * slab]

        for s in range(1, slices - 1):
            sweep(s)
        for side in range(2):
            halo(half, side).wait_recv()
            if half == 0:
                sigma_halo(side).wait_recv()
        for s in [-2, -1, 0, slices - 1, slices, slices + 1]:
            sweep(s)
        for s in range(-1, slices + 1):
            residue(s)
        for s in range(slices):
            finish(s)

    def send_back(half, steps):
        for step in steps:
            group = to_group(step)
            chosen = from_node_ref[pl.ds(pl.multiple_of(group * GROUP, GROUP), GROUP), :]
            rows = pl.ds(pl.multiple_of(group * LANES, LANES), LANES)
            back_ref[half, rows, :] = folded(dot(chosen, sol_ref[half]))
            send_group(back_ref, ret_ref, back_send, back_recv, half, step)

    def take_back(half):
        for k, step in enumerate(order):
            group_copy(back_ref, ret_ref, back_send, back_recv, half, step).wait_recv()
            source = from_group(step)
            got = ret_ref[half, pl.ds(pl.multiple_of(source * LANES, LANES), LANES), :]
            part = dot(from_slot_ref[source], pieces(got))
            mine_ref[...] = part if k == 0 else mine_ref[...] + part

    def lift(half):
        def lift_group(g, _):
            cols = pl.ds(pl.multiple_of(g * LANES, LANES), LANES)
            values = mine_ref[cols, :].T
            values = values[: LANES // 2] + values[LANES // 2 :]

            for k in range(BLOCK_EDGES // 8):
                rows = slice(k * 8, k * 8 + 8)

                def taken(c, ids, part):
                    found = None
                    for piece in range(NODE_BLOCK // 8):
                        start = c * NODE_BLOCK + piece * 8
                        here = jnp.take_along_axis(
                            values[start : start + 8], ids, axis=0, mode="promise_in_bounds"
                        )
                        found = here if piece == 0 else jnp.where(part == piece, here, found)
                    return found

                tails = ends_ref[0, rows, cols]
                heads = ends_ref[1, rows, cols]
                tail_at, tail_part = tails & 7, tails >> 3
                head_at, head_part = heads & 7, heads >> 3
                pair = taken(0, head_at, head_part) + taken(0, tail_at, tail_part)
                total = tangent_ref[2 * half, rows, cols] * pair
                if half:
                    drop = taken(1, head_at, head_part) - taken(1, tail_at, tail_part)
                    out_ref[rows, cols] = out_ref[rows, cols] + 0.5 * total + drop
                else:
                    pair = taken(1, head_at, head_part) + taken(1, tail_at, tail_part)
                    total = total + tangent_ref[1, rows, cols] * pair
                    out_ref[rows, cols] = 0.5 * total
            return 0

        lax.fori_loop(0, lane_groups, lift_group, 0)

    wide_sigma_ref[at_slices(0, slices, 2)] = sigma_ref[...]
    for load in loads:
        load.wait()
    find_terms(0)
    pl.semaphore_wait(barrier, n - 1)
    send_labels()
    send_terms(0, order)
    for side in range(2):
        sigma_halo(side).start()
    find_terms(1)
    send_terms(1, order[: groups // 2])
    prepare_return()
    take_labels()
    sum_terms(0)
    for side in range(2):
        halo(0, side).start()
    send_terms(1, order[groups // 2 :])
    smooth(0)
    send_back(0, order[: groups // 2])
    sum_terms(1)
    for side in range(2):
        halo(1, side).start()
    send_back(0, order[groups // 2 :])
    smooth(1)
    send_back(1, order)
    for half in range(2):
        take_back(half)
        lift(half)

    for half in range(2):
        for step in order:
            group_copy(send_ref, got_ref, go_send, go_recv, half, step).wait_send()
            group_copy(back_ref, ret_ref, back_send, back_recv, half, step).wait_send()
        for side in range(2):
            halo(half, side).wait_send()
    for side in range(2):
        sigma_halo(side).wait_send()


def per_device(n, n_node, residual, tangent, jacobi, ends, target, node_block, sigma):
    blocks = residual.shape[1]
    slices, rows_radial, rows_axial = sigma.shape
    nodal = slices * rows_radial * rows_axial // NODE_BLOCK // 2
    slots = 2 * blocks
    rows = slots // 2
    parts = sigma.reshape(slices, 2, LANES, NODE_BLOCK)
    inner, outer = (parts[:, k].reshape(nodal, NODE_BLOCK) for k in range(2))
    cells = jnp.concatenate([inner, inner, outer, outer], axis=1)
    groups = slots // GROUP
    vmem = pl.BlockSpec(memory_space=pltpu.VMEM)
    hbm = pl.BlockSpec(memory_space=pl.ANY)
    lifted = pl.pallas_call(
        functools.partial(kernel, n, n_node, slices),
        out_shape=jax.ShapeDtypeStruct(residual.shape, F32),
        in_specs=[hbm] * 3 + [vmem] * 3,
        out_specs=vmem,
        scratch_shapes=[
            pltpu.VMEM(residual.shape, F32),
            pltpu.VMEM(tangent.shape, F32),
            pltpu.VMEM(ends.shape, jnp.int32),
            pltpu.SemaphoreType.DMA((3,)),
            pltpu.VMEM((1, blocks), jnp.int32),
            pltpu.VMEM((blocks, LANES), F32),
            pltpu.VMEM((n, 1, GROUP), F32),
            pltpu.VMEM((n, 1, GROUP), F32),
            pltpu.VMEM((slots, blocks), BF16),
            pltpu.VMEM((groups, 2 * nodal, GROUP), BF16),
            pltpu.VMEM((slots, 2 * nodal), BF16),
            pltpu.VMEM((groups, blocks, GROUP), BF16),
            pltpu.VMEM((2, blocks, LANES), BF16),
            pltpu.VMEM((2, rows, LANES), F32),
            pltpu.VMEM((2, rows, LANES), F32),
            pltpu.VMEM((2 * nodal, LANES), F32),
            pltpu.VMEM((2, nodal + 6 * LANES, LANES), F32),
            pltpu.VMEM((nodal + 4 * LANES, LANES), F32),
            pltpu.VMEM((nodal + 4 * LANES, LANES), F32),
            pltpu.VMEM((nodal + 2 * LANES, LANES), F32),
            pltpu.VMEM((2, 2 * nodal, LANES), BF16),
            pltpu.VMEM((2, rows, LANES), F32),
            pltpu.VMEM((2, rows, LANES), F32),
            pltpu.VMEM((blocks, LANES), F32),
            pltpu.SemaphoreType.DMA,
            pltpu.SemaphoreType.DMA,
            pltpu.SemaphoreType.DMA((2, groups)),
            pltpu.SemaphoreType.DMA((2, groups)),
            pltpu.SemaphoreType.DMA((2, groups)),
            pltpu.SemaphoreType.DMA((2, groups)),
            pltpu.SemaphoreType.DMA((2, 2)),
            pltpu.SemaphoreType.DMA((2, 2)),
            pltpu.SemaphoreType.DMA((2,)),
            pltpu.SemaphoreType.DMA((2,)),
        ],
        compiler_params=pltpu.CompilerParams(
            collective_id=0, has_side_effects=True, vmem_limit_bytes=48 * 1024 * 1024
        ),
    )(
        residual,
        tangent,
        ends,
        target.T,
        node_block.reshape(1, blocks),
        cells,
    )
    return jacobi * residual + lifted


def solution(mesh):
    in_specs = (
        P(None, ("edge", "node")),
        P(None, None, ("edge", "node")),
        P(None, ("edge", "node")),
        P(None, None, ("edge", "node")),
        P(("edge", "node"), None),
        P(("edge", "node")),
        P(("edge", "node"), None, None),
    )
    out_specs = P(None, ("edge", "node"))
    n_node = mesh.shape["node"]
    n = mesh.shape["edge"] * n_node
    return jax.shard_map(
        functools.partial(per_device, n, n_node),
        mesh=mesh,
        in_specs=in_specs,
        out_specs=out_specs,
        check_vma=False,
    )
```

```python
import functools

import jax
import jax.numpy as jnp
from jax import lax
from jax.experimental import pallas as pl
from jax.experimental.pallas import tpu as pltpu
from jax.sharding import PartitionSpec as P

BLOCK_EDGES = 64
NODE_BLOCK = 32
LANES = 128
GROUP = 256

F32 = jnp.float32
BF16 = jnp.bfloat16
MESH = pl.DeviceIdType.MESH


def hot(mask):
    return jnp.where(mask, 1.0, 0.0).astype(BF16)


def dot(a, b):
    return jnp.dot(a, b, preferred_element_type=F32)


def left_lanes():
    return lax.broadcasted_iota(jnp.int32, (1, LANES), 1) < LANES // 2


def pieces(values):
    high = values.astype(BF16).astype(F32)
    low = values - high
    turn = LANES // 2
    upper = jnp.where(left_lanes(), high, pltpu.roll(low, turn, 1))
    lower = jnp.where(left_lanes(), pltpu.roll(high, turn, 1), low)
    return jnp.concatenate([upper, lower], axis=0).astype(BF16)


def folded(product):
    both = product + pltpu.roll(product, LANES // 2, 1)
    rows = product.shape[0] // 2
    return jnp.where(left_lanes(), both[:rows], both[rows:])


def order_of(groups):
    return [(groups // 2 + 3 * k) % groups for k in range(groups)]


def kernel(
    n,
    n_node,
    slices,
    resid_in,
    tangent_in,
    ends_in,
    target_ref,
    label_ref,
    sigma_ref,
    out_ref,
    resid_ref,
    tangent_ref,
    ends_ref,
    load_sem,
    pos_ref,
    posb_ref,
    lab_out,
    lab_in,
    to_slot_ref,
    to_node_ref,
    from_node_ref,
    from_slot_ref,
    rows_ref,
    send_ref,
    got_ref,
    acc_ref,
    source_ref,
    wide_sigma_ref,
    first_ref,
    rest_ref,
    sol_ref,
    back_ref,
    ret_ref,
    mine_ref,
    lab_send,
    lab_recv,
    go_send,
    go_recv,
    back_send,
    back_recv,
    halo_send,
    halo_recv,
    sigma_send,
    sigma_recv,
):
    me = lax.axis_index("edge") * n_node + lax.axis_index("node")
    blocks = resid_ref.shape[1]
    lane_groups = blocks // LANES
    cap = 2 * blocks // n
    deep = cap // 2
    peers = GROUP // cap
    groups = n // peers
    my_group = me // peers
    my_place = lax.rem(me, peers)
    slab = LANES
    nodal = slices * slab
    order = order_of(groups)

    def device(t):
        return (t // n_node, lax.rem(t, n_node))

    def to_group(step):
        return lax.rem(my_group + step, groups)

    def from_group(step):
        return lax.rem(my_group + groups - step, groups)

    def partner(group, turn):
        return group * peers + lax.rem(my_place + turn, peers)

    barrier = pltpu.get_barrier_semaphore()
    for step in range(1, n):
        pl.semaphore_signal(
            barrier, inc=1, device_id=device(lax.rem(me + step, n)), device_id_type=MESH
        )

    loads = [
        pltpu.make_async_copy(src, dst, load_sem.at[k])
        for k, (src, dst) in enumerate(
            ((resid_in, resid_ref), (ends_in, ends_ref), (tangent_in, tangent_ref))
        )
    ]
    for load in loads:
        load.start()

    upper = hot(
        lax.broadcasted_iota(jnp.int32, (LANES, LANES), 0)
        <= lax.broadcasted_iota(jnp.int32, (LANES, LANES), 1)
    )
    device_ids = lax.broadcasted_iota(jnp.int32, (n, LANES), 0)
    slot_ids = lax.broadcasted_iota(jnp.int32, (GROUP, LANES), 0)
    carry = jnp.zeros((n, 1), F32)
    label_sum = jnp.zeros((2 * n, GROUP), F32)
    offset = my_place * deep
    for g in range(lane_groups):
        cols = slice(g * LANES, (g + 1) * LANES)
        named = target_ref[:, cols]
        match = jnp.where(device_ids == named, 1.0, 0.0)
        local = dot(match.astype(BF16), upper)
        rank = jnp.sum(match * (local + carry), axis=0, keepdims=True) - 1.0
        carry = carry + local[:, LANES - 1 :]
        rank = rank.astype(jnp.int32)
        slot = jnp.where(rank < deep, rank, rank - deep + LANES)
        row = named * deep
        place = (row & (LANES - 1)) + 2 * (row - (row & (LANES - 1))) + slot
        pos_ref[:, cols] = place
        posb_ref[cols, :] = jnp.broadcast_to(place.astype(F32), (LANES, LANES)).T
        mark = label_ref[:, cols] + 1
        high = match * (mark >> 5).astype(F32)
        low = match * (mark & 31).astype(F32)
        label_sum = label_sum + lax.dot_general(
            jnp.concatenate([high, low], axis=0).astype(BF16),
            hot(slot_ids == slot + offset),
            (((1,), (1,)), ((), ())),
            preferred_element_type=F32,
        )
    labels = 32.0 * label_sum[:n] + label_sum[n:]
    for t in range(n):
        lab_out[t] = labels[t : t + 1]

    def send_labels():
        lab_in[me] = lab_out[me]
        for step in range(1, n):
            t = lax.rem(me + step, n)
            pltpu.make_async_remote_copy(
                src_ref=lab_out.at[t],
                dst_ref=lab_in.at[me],
                send_sem=lab_send,
                recv_sem=lab_recv,
                device_id=device(t),
                device_id_type=MESH,
            ).start()

    node_ids = lax.broadcasted_iota(jnp.int32, (NODE_BLOCK, LANES), 0)

    def find_terms(half):
        def terms_of(g, _):
            cols = pl.ds(pl.multiple_of(g * LANES, LANES), LANES)

            def chunk(k, sums):
                rows = pl.ds(pl.multiple_of(k * 8, 8), 8)
                residual = resid_ref[rows, cols]
                halved = 0.5 * residual
                vectors = [
                    tangent_ref[c, rows, cols] * halved for c in range(2 * half, min(3, 2 * half + 2))
                ]
                tails = ends_ref[0, rows, cols]
                heads = ends_ref[1, rows, cols]
                sums = list(sums)
                for e in range(8):
                    at_tail = node_ids == tails[e : e + 1]
                    at_head = node_ids == heads[e : e + 1]
                    either = at_tail | at_head
                    for c, vector in enumerate(vectors):
                        sums[c] = sums[c] + jnp.where(either, vector[e : e + 1], 0.0)
                    if half:
                        value = residual[e : e + 1]
                        sums[1] = sums[1] + jnp.where(
                            at_head, value, jnp.where(at_tail, -value, 0.0)
                        )
                return tuple(sums)

            zero = jnp.zeros((NODE_BLOCK, LANES), F32)
            sums = lax.fori_loop(0, BLOCK_EDGES // 8, chunk, (zero,) * 2)
            high = [total.astype(BF16).astype(F32) for total in sums]
            low = [total - part for total, part in zip(sums, high)]
            rows_ref[half, cols, :] = jnp.concatenate(high + low, axis=0).T.astype(BF16)
            return 0

        lax.fori_loop(0, lane_groups, terms_of, 0)

    def rows_copy(src, dst, sends, recvs, half, step, turn):
        t = partner(to_group(step), turn)
        return pltpu.make_async_remote_copy(
            src_ref=src.at[half, pl.ds(pl.multiple_of(t * deep, deep), deep)],
            dst_ref=dst.at[half, pl.ds(pl.multiple_of(me * deep, deep), deep)],
            send_sem=sends.at[half, step],
            recv_sem=recvs.at[half, step],
            device_id=device(t),
            device_id_type=MESH,
        )

    def group_copy(src, dst, sends, recvs, half, step):
        size = LANES if step else LANES - deep
        return pltpu.make_async_remote_copy(
            src_ref=src.at[half, pl.ds(0, size)],
            dst_ref=dst.at[half, pl.ds(0, size)],
            send_sem=sends.at[half, step],
            recv_sem=recvs.at[half, step],
            device_id=device(me),
            device_id_type=MESH,
        )

    def send_group(src, dst, sends, recvs, half, step):
        for turn in range(peers):
            if step == 0 and turn == 0:
                mine = pl.ds(pl.multiple_of(me * deep, deep), deep)
                dst[half, mine, :] = src[half, mine, :]
            else:
                rows_copy(src, dst, sends, recvs, half, step, turn).start()

    row_ids = lax.broadcasted_iota(jnp.int32, (GROUP, blocks), 0)

    def send_terms(half, steps):
        for step in steps:
            group = to_group(step)
            at = pl.ds(pl.multiple_of(group * GROUP, GROUP), GROUP)
            if half == 0:
                chosen = hot(pos_ref[...] - group * GROUP == row_ids)
                to_slot_ref[at, :] = chosen
            else:
                chosen = to_slot_ref[at, :]
            rows = pl.ds(pl.multiple_of(group * LANES, LANES), LANES)
            send_ref[half, rows, :] = folded(dot(chosen, rows_ref[half]))
            send_group(send_ref, got_ref, go_send, go_recv, half, step)

    slot_lanes = lax.broadcasted_iota(jnp.int32, (blocks, LANES), 1).astype(F32)

    def prepare_return():
        for g in range(groups):
            for part in range(2):
                lanes = slice(part * LANES, (part + 1) * LANES)
                ids = slot_lanes + float(g * GROUP + part * LANES)
                from_slot_ref[g, :, lanes] = hot(posb_ref[...] == ids)

    def label_row(group):
        total = lab_in[group * peers]
        for k in range(1, peers):
            total = total + lab_in[group * peers + k]
        return total

    def take_labels():
        pltpu.make_async_remote_copy(
            src_ref=lab_out.at[pl.ds(0, n - 1)],
            dst_ref=lab_in.at[pl.ds(0, n - 1)],
            send_sem=lab_send,
            recv_sem=lab_recv,
            device_id=device(me),
            device_id_type=MESH,
        ).wait()
        for g in range(groups):
            row = label_row(g)
            for part in range(2):
                lanes = slice(part * LANES, (part + 1) * LANES)
                marks = row[:, lanes]
                for side in range(2):
                    rows = slice(side * nodal, (side + 1) * nodal)
                    to_node_ref[g, rows, lanes] = hot(block_ids(side) == marks)
        for g in range(groups):
            row = label_row(g)
            for part in range(2):
                start = g * GROUP + part * LANES
                marks = row[:, part * LANES : (part + 1) * LANES]
                marks = jnp.broadcast_to(marks, (LANES, LANES)).T
                for side in range(2):
                    for s in range(slices):
                        column = side * nodal + s * slab
                        from_node_ref[start : start + LANES, column : column + slab] = hot(
                            marks == lane_ids + float((2 * s + side) * slab + 1)
                        )

    def block_ids(side):
        rows = lax.broadcasted_iota(jnp.int32, (slab, LANES), 0)
        return jnp.concatenate(
            [(rows + (2 * s + side) * slab + 1).astype(F32) for s in range(slices)], axis=0
        )

    lane_ids = lax.broadcasted_iota(jnp.int32, (LANES, LANES), 1).astype(F32)

    def sum_terms(half):
        for k, step in enumerate(order):
            group_copy(send_ref, got_ref, go_send, go_recv, half, step).wait_recv()
            source = from_group(step)
            got = got_ref[half, pl.ds(pl.multiple_of(source * LANES, LANES), LANES), :]
            part = dot(to_node_ref[source], pieces(got))
            acc_ref[...] = part if k == 0 else acc_ref[...] + part
        source_ref[half, at_slices(0, slices, 3)] = folded(acc_ref[...])

    inner = lax.broadcasted_iota(jnp.int32, (slab, LANES), 0) & 7
    node = lax.broadcasted_iota(jnp.int32, (slab, LANES), 1) & (NODE_BLOCK - 1)
    last_node = node == NODE_BLOCK - 1
    first_node = node == 0
    last_inner = inner == 7
    first_inner = inner == 0
    left = lax.rem(me + n - 1, n)
    right = lax.rem(me + 1, n)

    def at_slices(first, last, margin):
        return slice((first + margin) * slab, (last + margin) * slab)

    def halo(half, side):
        at = at_slices(0, 3, 3) if side == 0 else at_slices(slices - 3, slices, 3)
        to = at_slices(slices, slices + 3, 3) if side == 0 else at_slices(-3, 0, 3)
        return pltpu.make_async_remote_copy(
            src_ref=source_ref.at[half, at],
            dst_ref=source_ref.at[half, to],
            send_sem=halo_send.at[half, side],
            recv_sem=halo_recv.at[half, side],
            device_id=device(left if side == 0 else right),
            device_id_type=MESH,
        )

    def sigma_halo(side):
        at = at_slices(0, 2, 2) if side == 0 else at_slices(slices - 2, slices, 2)
        to = at_slices(slices, slices + 2, 2) if side == 0 else at_slices(-2, 0, 2)
        return pltpu.make_async_remote_copy(
            src_ref=wide_sigma_ref.at[at],
            dst_ref=wide_sigma_ref.at[to],
            send_sem=sigma_send.at[side],
            recv_sem=sigma_recv.at[side],
            device_id=device(left if side == 0 else right),
            device_id_type=MESH,
        )

    def smooth(half):
        lane = lax.broadcasted_iota(jnp.int32, (1, LANES), 1)
        scale = jnp.where((lane & (LANES // 2 - 1)) < NODE_BLOCK, 1.0, 0.5 if half else 1.0)
        scale = scale.astype(F32)
        top = 12.0 + 8.0 * scale
        bottom = top / 8.0
        centre = (top + bottom) / 2.0
        radius = (top - bottom) / 2.0
        ratio = centre / radius
        first = 1.0 / ratio
        second = 1.0 / (2.0 * ratio - first)
        coef_one = second * first
        coef_two = 2.0 * second / radius
        inverse = 1.0 / centre
        source = source_ref.at[half]

        def applied(field, margin, s):
            here = field[at_slices(s, s + 1, margin)]
            beside = field[at_slices(s - 1, s, margin)] + field[at_slices(s + 1, s + 2, margin)]
            turn = LANES // 2
            inward = jnp.where(left_lanes(), 0.0, pltpu.roll(here[-8:], turn, 1))
            outward = jnp.where(left_lanes(), pltpu.roll(here[:8], turn, 1), 0.0)
            beside = beside + jnp.concatenate([inward, here[:-8]], axis=0)
            beside = beside + jnp.concatenate([here[8:], outward], axis=0)
            after = pltpu.roll(pltpu.roll(here, slab - 1, 0), NODE_BLOCK - 1, 1)
            after = jnp.where(last_inner, 0.0, after)
            before = pltpu.roll(pltpu.roll(here, 1, 0), LANES - NODE_BLOCK + 1, 1)
            before = jnp.where(first_inner, 0.0, before)
            beside = beside + jnp.where(last_node, after, pltpu.roll(here, LANES - 1, 1))
            beside = beside + jnp.where(first_node, before, pltpu.roll(here, 1, 1))
            diag = 6.0 + scale * wide_sigma_ref[at_slices(s, s + 1, 2)]
            return here, diag * here - beside

        def sweep(s):
            here, image = applied(source, 3, s)
            step = here * inverse
            first_ref[at_slices(s, s + 1, 2)] = step + (
                coef_one * step + coef_two * (here - image * inverse)
            )

        def residue(s):
            image = applied(first_ref, 2, s)[1]
            rest_ref[at_slices(s, s + 1, 1)] = source[at_slices(s, s + 1, 3)] - image

        def finish(s):
            here, image = applied(rest_ref, 1, s)
            step = here * inverse
            total = (first_ref[at_slices(s, s + 1, 2)] + step) + (
                coef_one * step + coef_two * (here - image * inverse)
            )
            parts = pieces(total)
            for side in range(2):
                start = side * nodal + s * slab
                sol_ref[half, start : start + slab, :] = parts[side * slab : (side + 1) * slab]

        for s in range(1, slices - 1):
            sweep(s)
        for side in range(2):
            halo(half, side).wait_recv()
            if half == 0:
                sigma_halo(side).wait_recv()
        for s in [-2, -1, 0, slices - 1, slices, slices + 1]:
            sweep(s)
        for s in range(-1, slices + 1):
            residue(s)
        for s in range(slices):
            finish(s)

    def send_back(half, steps):
        for step in steps:
            group = to_group(step)
            chosen = from_node_ref[pl.ds(pl.multiple_of(group * GROUP, GROUP), GROUP), :]
            rows = pl.ds(pl.multiple_of(group * LANES, LANES), LANES)
            back_ref[half, rows, :] = folded(dot(chosen, sol_ref[half]))
            send_group(back_ref, ret_ref, back_send, back_recv, half, step)

    def take_back(half):
        for k, step in enumerate(order):
            group_copy(back_ref, ret_ref, back_send, back_recv, half, step).wait_recv()
            source = from_group(step)
            got = ret_ref[half, pl.ds(pl.multiple_of(source * LANES, LANES), LANES), :]
            part = dot(from_slot_ref[source], pieces(got))
            mine_ref[...] = part if k == 0 else mine_ref[...] + part

    def lift(half):
        def lift_group(g, _):
            cols = pl.ds(pl.multiple_of(g * LANES, LANES), LANES)
            values = mine_ref[cols, :].T
            values = values[: LANES // 2] + values[LANES // 2 :]

            for k in range(BLOCK_EDGES // 8):
                rows = slice(k * 8, k * 8 + 8)

                def taken(c, ids, part):
                    found = None
                    for piece in range(NODE_BLOCK // 8):
                        start = c * NODE_BLOCK + piece * 8
                        here = jnp.take_along_axis(
                            values[start : start + 8], ids, axis=0, mode="promise_in_bounds"
                        )
                        found = here if piece == 0 else jnp.where(part == piece, here, found)
                    return found

                tails = ends_ref[0, rows, cols]
                heads = ends_ref[1, rows, cols]
                tail_at, tail_part = tails & 7, tails >> 3
                head_at, head_part = heads & 7, heads >> 3
                pair = taken(0, head_at, head_part) + taken(0, tail_at, tail_part)
                total = tangent_ref[2 * half, rows, cols] * pair
                if half:
                    drop = taken(1, head_at, head_part) - taken(1, tail_at, tail_part)
                    out_ref[rows, cols] = out_ref[rows, cols] + 0.5 * total + drop
                else:
                    pair = taken(1, head_at, head_part) + taken(1, tail_at, tail_part)
                    total = total + tangent_ref[1, rows, cols] * pair
                    out_ref[rows, cols] = 0.5 * total
            return 0

        lax.fori_loop(0, lane_groups, lift_group, 0)

    lane = lax.broadcasted_iota(jnp.int32, (1, LANES), 1)
    radial = sigma_ref.shape[1] // 2
    for s in range(slices):
        for k in range(8):
            first_lane = k * NODE_BLOCK % LANES
            at = slice(k * NODE_BLOCK // LANES * LANES, k * NODE_BLOCK // LANES * LANES + LANES)
            cells = sigma_ref[s, :, at]
            if first_lane:
                cells = pltpu.roll(cells, LANES - first_lane, 1)
            cells = jnp.where(lane < NODE_BLOCK, cells, 0.0)
            cells = cells + pltpu.roll(cells, NODE_BLOCK, 1)
            cells = cells[:radial] + pltpu.roll(cells[radial:], LANES // 2, 1)
            wide_sigma_ref[pl.ds((s + 2) * slab + k, radial, stride=8), :] = cells
    for load in loads:
        load.wait()
    find_terms(0)
    pl.semaphore_wait(barrier, n - 1)
    send_labels()
    send_terms(0, order)
    for side in range(2):
        sigma_halo(side).start()
    find_terms(1)
    send_terms(1, order[: groups // 4])
    prepare_return()
    take_labels()
    sum_terms(0)
    for side in range(2):
        halo(0, side).start()
    send_terms(1, order[groups // 4 :])
    smooth(0)
    send_back(0, order[: groups // 4])
    sum_terms(1)
    for side in range(2):
        halo(1, side).start()
    send_back(0, order[groups // 4 :])
    smooth(1)
    send_back(1, order)
    for half in range(2):
        take_back(half)
        lift(half)

    for half in range(2):
        for step in order:
            group_copy(send_ref, got_ref, go_send, go_recv, half, step).wait_send()
            group_copy(back_ref, ret_ref, back_send, back_recv, half, step).wait_send()
        for side in range(2):
            halo(half, side).wait_send()
    for side in range(2):
        sigma_halo(side).wait_send()


def per_device(n, n_node, residual, tangent, jacobi, ends, target, node_block, sigma):
    blocks = residual.shape[1]
    slices, rows_radial, rows_axial = sigma.shape
    nodal = slices * rows_radial * rows_axial // NODE_BLOCK // 2
    slots = 2 * blocks
    rows = slots // 2
    groups = slots // GROUP
    vmem = pl.BlockSpec(memory_space=pltpu.VMEM)
    hbm = pl.BlockSpec(memory_space=pltpu.HBM)
    lifted = pl.pallas_call(
        functools.partial(kernel, n, n_node, slices),
        out_shape=jax.ShapeDtypeStruct(residual.shape, F32),
        in_specs=[hbm] * 3 + [vmem] * 3,
        out_specs=vmem,
        scratch_shapes=[
            pltpu.VMEM(residual.shape, F32),
            pltpu.VMEM(tangent.shape, F32),
            pltpu.VMEM(ends.shape, jnp.int32),
            pltpu.SemaphoreType.DMA((3,)),
            pltpu.VMEM((1, blocks), jnp.int32),
            pltpu.VMEM((blocks, LANES), F32),
            pltpu.VMEM((n, 1, GROUP), F32),
            pltpu.VMEM((n, 1, GROUP), F32),
            pltpu.VMEM((slots, blocks), BF16),
            pltpu.VMEM((groups, 2 * nodal, GROUP), BF16),
            pltpu.VMEM((slots, 2 * nodal), BF16),
            pltpu.VMEM((groups, blocks, GROUP), BF16),
            pltpu.VMEM((2, blocks, LANES), BF16),
            pltpu.VMEM((2, rows, LANES), F32),
            pltpu.VMEM((2, rows, LANES), F32),
            pltpu.VMEM((2 * nodal, LANES), F32),
            pltpu.VMEM((2, nodal + 6 * LANES, LANES), F32),
            pltpu.VMEM((nodal + 4 * LANES, LANES), F32),
            pltpu.VMEM((nodal + 4 * LANES, LANES), F32),
            pltpu.VMEM((nodal + 2 * LANES, LANES), F32),
            pltpu.VMEM((2, 2 * nodal, LANES), BF16),
            pltpu.VMEM((2, rows, LANES), F32),
            pltpu.VMEM((2, rows, LANES), F32),
            pltpu.VMEM((blocks, LANES), F32),
            pltpu.SemaphoreType.DMA,
            pltpu.SemaphoreType.DMA,
            pltpu.SemaphoreType.DMA((2, groups)),
            pltpu.SemaphoreType.DMA((2, groups)),
            pltpu.SemaphoreType.DMA((2, groups)),
            pltpu.SemaphoreType.DMA((2, groups)),
            pltpu.SemaphoreType.DMA((2, 2)),
            pltpu.SemaphoreType.DMA((2, 2)),
            pltpu.SemaphoreType.DMA((2,)),
            pltpu.SemaphoreType.DMA((2,)),
        ],
        compiler_params=pltpu.CompilerParams(
            collective_id=0, has_side_effects=True, vmem_limit_bytes=63 * 1024 * 1024
        ),
    )(
        residual,
        tangent,
        ends,
        target.T,
        node_block.reshape(1, blocks),
        sigma,
    )
    return jacobi * residual + lifted


def solution(mesh):
    in_specs = (
        P(None, ("edge", "node")),
        P(None, None, ("edge", "node")),
        P(None, ("edge", "node")),
        P(None, None, ("edge", "node")),
        P(("edge", "node"), None),
        P(("edge", "node")),
        P(("edge", "node"), None, None),
    )
    out_specs = P(None, ("edge", "node"))
    n_node = mesh.shape["node"]
    n = mesh.shape["edge"] * n_node
    return jax.shard_map(
        functools.partial(per_device, n, n_node),
        mesh=mesh,
        in_specs=in_specs,
        out_specs=out_specs,
        check_vma=False,
    )
```
